256 devices in a mesh: gx: 16 (over x, y), gy: 8 (over z), gz: 2 (over core).
Axes of the slice: x: 4, y: 4, z: 8, core: 2. Of those that a mesh axis runs over, the one named last changes fastest.
Arguments:
- state: float32 [64, 32, 5, 15, 256], P('gx', 'gy', None, None, 'gz'), may hold values from -0.75 to 0.75
- source: float32 [64, 32, 5, 15, 256], P('gx', 'gy', None, None, 'gz'), may hold values from -0.75 to 0.75
- x_faces: float32 [2, 64, 32, 5, 256], P(None, 'gx', 'gy', None, 'gz'), may hold values from 1 to 4
- y_faces: float32 [2, 64, 32, 5, 256], P(None, 'gx', 'gy', None, 'gz'), may hold values from 1 to 4
- couple: float32 [64, 32, 5, 5, 256], P('gx', 'gy', None, None, 'gz'), may hold values from -0.004 to 0.03, as said below
- omega: float32 [1], replicated, may hold values from 0.5 to 1.5
Outputs:
- new_state: float32 [64, 32, 5, 15, 256], P('gx', 'gy', None, None, 'gz')
The draws below stay inside these ranges and needn't reach their ends.
Inputs may be any that keep to these rules, and one draw needn't show every extreme that they name: In every 5 x 5 block of couple each diagonal entry is positive and exceeds the sum of magnitudes of the other entries of its row.
All inputs are finite; a program needn't handle non-finite values.
Results may differ from the reference program's by a relative error of at most 0.0003.
Values sent between devices are 32-bit elements; how exact they have to be, the bound alone decides.
No kernel may reach another device: no remote copies, remote signals or barrier semaphores. Data moves between devices by JAX's collectives and lax.ppermute only.
A program may use at most 64 MiB of HBM per device.

```python
import math
import jax
import jax.numpy as jnp
from jax import lax

VARS = 5
INST = 15
NX = 64
NY = 32
NZ = 256


def draw_couple(key, part):
    first_key, second_key = jax.random.split(key)
    shape = (NX, NY, VARS, VARS, NZ)
    spread = jax.random.uniform(first_key, shape, jnp.float32, -0.003, 0.001)
    margin = jnp.exp(jax.random.uniform(second_key, (NX, NY, VARS, NZ), jnp.float32, math.log(0.001), math.log(0.015)))
    ident = jnp.eye(VARS, dtype=jnp.float32)[None, None, :, :, None]
    spread = spread * (1.0 - ident)
    dominance = jnp.sum(jnp.abs(spread), axis=3) + margin
    return spread + dominance[:, :, :, None, :] * ident


def block_scale(own_key, shape, cuts, least, largest):
    def one(axis_at, shards_of):
        steps = jax.random.uniform(jax.random.fold_in(jax.random.fold_in(own_key, 6), axis_at), (shards_of,), jnp.float32, least / len(cuts), largest / len(cuts))
        return jnp.repeat(jnp.exp(steps), shape[axis_at] // shards_of).reshape((-1,) + (1,) * (len(shape) - axis_at - 1))

    factor_of = one(*cuts[0])
    for cut in cuts[1:]:
        factor_of = factor_of * one(*cut)
    return factor_of


def bell_draw(own_key, dims, scale, limit, pieces=(), kind=jnp.bfloat16):
    level = block_scale(own_key, dims, pieces, -0.22, 0.18) if pieces else 1.0
    values = jax.random.normal(own_key, dims, jnp.float32) * scale * level
    return jnp.minimum(jnp.maximum(values, -limit), limit).astype(kind)


def setup_inputs(seed: int = 0) -> dict:
    streams_of = jax.random.split(jax.random.key(seed), 7)
    return {
        "state": bell_draw(streams_of[0], (NX, NY, VARS, INST, NZ), 0.05, 0.75, ((0, 16), (1, 8), (4, 2)), jnp.float32),
        "source": bell_draw(streams_of[1], (NX, NY, VARS, INST, NZ), 0.05, 0.75, ((0, 16), (1, 8), (4, 2)), jnp.float32),
        "x_faces": jnp.clip(jnp.exp(math.log(4.0) - 1.3862944 * jax.random.uniform(streams_of[2], (2, NX, NY, VARS, NZ), jnp.float32) ** block_scale(streams_of[2], (2, NX, NY, VARS, NZ), ((1, 16), (2, 8), (4, 2)), -0.2, 0.2)), 1.0, 4.0),
        "y_faces": jnp.clip(jnp.exp(math.log(4.0) - 1.3862944 * jax.random.uniform(streams_of[3], (2, NX, NY, VARS, NZ), jnp.float32) ** block_scale(streams_of[3], (2, NX, NY, VARS, NZ), ((1, 16), (2, 8), (4, 2)), -0.2, 0.2)), 1.0, 4.0),
        "couple": draw_couple(jax.random.fold_in(streams_of[6], 71), 0),
        "omega": jnp.clip(jax.random.uniform(streams_of[5], (1,), jnp.float32, 0.5, 1.5), 0.5, 1.5),
    }


z_weight = 0.5
highest = lax.Precision.HIGHEST


def product(left, right):
    return jnp.sum(left[..., :, :, None, :] * right[..., None, :, :, :], axis=-3)


def solve_block(matrix, right_side):
    width = matrix.shape[-2]
    matrix_rows = [matrix[..., row_number, :, :] for row_number in range(width)]
    right_rows = [right_side[..., row_number, :, :] for row_number in range(width)]
    for pivot_number in range(width):
        scaling = 1.0 / matrix_rows[pivot_number][..., pivot_number:pivot_number + 1, :]
        matrix_rows[pivot_number] = matrix_rows[pivot_number] * scaling
        right_rows[pivot_number] = right_rows[pivot_number] * scaling
        for row_number in range(width):
            if row_number != pivot_number:
                factor = matrix_rows[row_number][..., pivot_number:pivot_number + 1, :]
                matrix_rows[row_number] = matrix_rows[row_number] - factor * matrix_rows[pivot_number]
                right_rows[row_number] = right_rows[row_number] - factor * right_rows[pivot_number]
    return jnp.stack(right_rows, axis=-3)


def thomas_scan(low_blocks, mid_blocks, up_blocks, right_side):
    width = mid_blocks.shape[-2]

    def forward(carry, items):
        factor_prev, value_prev = carry
        low_blk, mid_blk, up_blk, right_blk = items
        pivot_blk = mid_blk - product(low_blk, factor_prev)
        joined = solve_block(pivot_blk, jnp.concatenate([up_blk, right_blk - product(low_blk, value_prev)], axis=-2))
        factor_now = joined[..., :width, :]
        value_now = joined[..., width:, :]
        return (factor_now, value_now), (factor_now, value_now)

    start = (jnp.zeros_like(mid_blocks[0]), jnp.zeros_like(right_side[0]))
    _, (factors, values) = lax.scan(forward, start, (low_blocks, mid_blocks, up_blocks, right_side))

    def backward(after, items):
        factor_now, value_now = items
        result = value_now - product(factor_now, after)
        return result, result

    _, results = lax.scan(backward, jnp.zeros_like(right_side[0]), (factors, values), reverse=True)
    return results


def spectral_table(inst_count):
    offsets = jnp.arange(inst_count, dtype=jnp.int32)
    gaps = offsets[:, None] - offsets[None, :]
    signs = jnp.where(gaps % 2 == 0, 1.0, -1.0).astype(jnp.float32)
    angles = math.pi * gaps.astype(jnp.float32) / inst_count
    safe_sine = jnp.where(gaps == 0, 1.0, jnp.sin(angles))
    return jnp.where(gaps == 0, 0.0, 0.5 * signs / safe_sine).astype(jnp.float32)


def residual(state, source, x_faces, y_faces, couple, omega, spectral):
    padded = jnp.pad(state, ((1, 1), (1, 1), (0, 0), (0, 0), (1, 1)))
    center = state
    x_low = x_faces[0][:, :, :, None, :]
    x_high = x_faces[1][:, :, :, None, :]
    y_low = y_faces[0][:, :, :, None, :]
    y_high = y_faces[1][:, :, :, None, :]
    applied = (x_low + x_high + y_low + y_high + 2.0 * z_weight) * center
    applied = applied - x_low * padded[:-2, 1:-1, :, :, 1:-1] - x_high * padded[2:, 1:-1, :, :, 1:-1]
    applied = applied - y_low * padded[1:-1, :-2, :, :, 1:-1] - y_high * padded[1:-1, 2:, :, :, 1:-1]
    applied = applied - z_weight * (padded[1:-1, 1:-1, :, :, :-2] + padded[1:-1, 1:-1, :, :, 2:])
    applied = applied + product(couple, center)
    applied = applied + omega[0] * jnp.einsum("jk,xyckz->xycjz", spectral, center, precision=highest)
    return source - applied


def line_update(low_faces, high_faces, couple, right_side):
    width = couple.shape[2]
    ident = jnp.eye(width, dtype=jnp.float32)[None, None, :, :, None]
    low_blocks = -low_faces[:, :, :, None, :] * ident
    up_blocks = -high_faces[:, :, :, None, :] * ident
    mid_blocks = (low_faces + high_faces)[:, :, :, None, :] * ident + couple
    return thomas_scan(low_blocks, mid_blocks, up_blocks, right_side)


def reference(state, source, x_faces, y_faces, couple, omega):
    spectral = spectral_table(state.shape[3])
    first_residual = residual(state, source, x_faces, y_faces, couple, omega, spectral)
    x_update = line_update(x_faces[0], x_faces[1], couple, first_residual)
    half_state = state + x_update
    second_residual = residual(half_state, source, x_faces, y_faces, couple, omega, spectral)
    y_update = line_update(jnp.moveaxis(y_faces[0], 1, 0), jnp.moveaxis(y_faces[1], 1, 0),
                           jnp.moveaxis(couple, 1, 0), jnp.moveaxis(second_residual, 1, 0))
    return half_state + jnp.moveaxis(y_update, 0, 1)
```

```python
import functools
import math

import jax
import jax.numpy as jnp
import numpy as np
from jax import lax
from jax.experimental import pallas as pl
from jax.experimental.pallas import tpu as pltpu
from jax.sharding import PartitionSpec as P


V = 5
N = 15
B = 4
H = 8
XR = 96
MR = 56
YR = 80
YM = 112
f32 = jnp.float32


def spectral_columns():
    offsets = np.arange(N)
    gaps = offsets[:, None] - offsets[None, :]
    signs = np.where(gaps % 2 == 0, 1.0, -1.0)
    sine = np.where(gaps == 0, 1.0, np.sin(math.pi * gaps / N))
    table = np.where(gaps == 0, 0.0, 0.5 * signs / sine).astype(np.float32)
    return np.ascontiguousarray(np.broadcast_to(table.T[:, :, None], (N, N, 128)))


def lane(shape=(8, 128)):
    return lax.broadcasted_iota(jnp.int32, shape, len(shape) - 1)


def sub(shape=(8, 128)):
    return lax.broadcasted_iota(jnp.int32, shape, len(shape) - 2)


def swap(v):
    return pltpu.roll(v, 64, 1)


def inverse(m):
    m = list(m)
    for p in range(V):
        piv = 1.0 / m[p * V + p]
        for j in range(V):
            if j != p:
                m[p * V + j] = m[p * V + j] * piv
        m[p * V + p] = piv
        for i in range(V):
            if i != p:
                f = m[i * V + p]
                for j in range(V):
                    if j != p:
                        m[i * V + j] = m[i * V + j] - f * m[p * V + j]
                m[i * V + p] = -f * piv
    return m


def dot(terms):
    total = None
    for a, b in terms:
        total = a * b if total is None else total + a * b
    return total


def matmul(a, b):
    return [
        dot([(a[i * V + k], b[k * V + j]) for k in range(V)]) for i in range(V) for j in range(V)
    ]


def pack_edges(load, flag):
    shift = jnp.where(flag == 0, 1, 0)
    lanes = lane((N, 128))
    acc = jnp.zeros((N, 128), f32)
    for c in range(B * B * V):
        x, y, i = c // (B * V), (c // V) % B, c % V
        acc = jnp.where(lanes == c, pltpu.roll(load(x, y, i), shift + c, 1), acc)
    return acc


def edge_kernel(flag_ref, state_ref, first_ref, last_ref, lanes_ref):
    first_ref[...] = state_ref[:, 0]
    last_ref[...] = state_ref[:, B - 1]
    lanes_ref[...] = pack_edges(lambda x, y, i: state_ref[x, y, i], flag_ref[0])


def z_neighbours(v, halo, c, flag, lanes):
    edge = jnp.where(flag == 0, 127, 0)
    low = jnp.where(lanes == 0, 0.0, pltpu.roll(v, 1, 1))
    high = jnp.where(lanes == 127, 0.0, pltpu.roll(v, 127, 1))
    shift = jnp.where(flag == 0, 127 - c, 128 - c)
    far = jnp.where(lanes == edge, pltpu.roll(halo, shift, 1), 0.0)
    return low + high + far


def matrix_kernel(couple_ref, xf_ref, yf_ref, fac_ref, xmat_ref, ymat_ref, mel, lo, hi):
    for a in range(B):
        for b in range(B):
            for i in range(V):
                c = couple_ref[a, b, i]
                mel[pl.ds((a * 25 + i * V) * 8 + b, V, stride=8), :] = c
                mel[pl.ds((b * 25 + i * V) * 8 + 4 + a, V, stride=8), :] = c
            lo[pl.ds(a * V * 8 + b, V, stride=8), :] = xf_ref[0, a, b]
            hi[pl.ds(a * V * 8 + b, V, stride=8), :] = xf_ref[1, a, b]
            lo[pl.ds(b * V * 8 + 4 + a, V, stride=8), :] = yf_ref[0, a, b]
            hi[pl.ds(b * V * 8 + 4 + a, V, stride=8), :] = yf_ref[1, a, b]

    def row(ref, r):
        return ref[r * 8 : r * 8 + 8, :]

    low = [[row(lo, t * V + i) for i in range(V)] for t in range(B)]
    high = [[row(hi, t * V + i) for i in range(V)] for t in range(B)]

    def mid(t):
        m = [row(mel, t * 25 + e) for e in range(25)]
        for i in range(V):
            m[i * V + i] = m[i * V + i] + (low[t][i] + high[t][i])
        return m

    def put(block, m):
        for e in range(25):
            fac_ref[block * 25 + e] = m[e]

    def get(block):
        return [fac_ref[block * 25 + e] for e in range(25)]

    def rows_by(d, m):
        return [d[i] * m[i * V + j] for i in range(V) for j in range(V)]

    def cols_by(m, d):
        return [m[i * V + j] * d[j] for i in range(V) for j in range(V)]

    g0 = inverse(mid(0))
    put(0, g0)
    m1 = mid(1)
    s = rows_by(low[1], cols_by(g0, high[0]))
    g1 = inverse([p - q for p, q in zip(m1, s)])
    put(1, g1)
    m2 = mid(2)
    s = rows_by(low[2], cols_by(g1, high[1]))
    g2 = inverse([p - q for p, q in zip(m2, s)])
    put(2, g2)
    e2 = cols_by(g2, high[2])
    put(8, e2)
    e1 = matmul(get(1), rows_by(high[1], e2))
    put(7, e1)
    e0 = matmul(get(0), rows_by(high[0], e1))
    put(6, e0)
    l0 = cols_by(get(0), low[0])
    l1 = matmul(get(1), rows_by(low[1], l0))
    l2 = matmul(get(2), rows_by(low[2], l1))
    put(5, l2)
    b1 = matmul(get(1), rows_by(high[1], l2))
    l1 = [p + q for p, q in zip(l1, b1)]
    put(4, l1)
    b0 = matmul(get(0), rows_by(high[0], l1))
    l0 = [p + q for p, q in zip(cols_by(get(0), low[0]), b0)]
    put(3, l0)

    lanes = lane()
    m3 = mid(3)
    last_low, last_high = get(5), get(8)
    first_low, first_high = get(3), get(6)

    def x_pair(r, e0, e1):
        for zh in range(2):
            if zh == 0:
                v = jnp.where(lanes < 64, e0, swap(e1))
            else:
                v = jnp.where(lanes < 64, swap(e0), e1)
            for ih in range(2):
                xmat_ref[pl.ds((zh * 2 + ih) * MR + r, 4, stride=4 * MR), :] = v[0:4]

    def y_row(r, e):
        ymat_ref[pl.ds(r, 4, stride=YM), :] = e[4:8]

    for i in range(V):
        for j in range(V):
            e = i * V + j
            a = -(low[3][i] * last_low[e])
            bb = m3[e] - low[3][i] * last_high[e]
            x_pair(e, a, first_high[e])
            x_pair(25 + e, bb, first_low[e])
            y_row(e, a)
            y_row(25 + e, bb)
            y_row(50 + e, first_low[e])
            y_row(75 + e, first_high[e])
        x_pair(50 + i, high[3][i], high[3][i])
        y_row(100 + i, high[3][i])
    for r in range(105, YM):
        y_row(r, jnp.zeros((8, 128), f32))
    x_pair(55, jnp.zeros((8, 128), f32), jnp.zeros((8, 128), f32))


def halves(v):
    return v[0:H], jnp.concatenate([v[H:N], jnp.zeros((1, 128), f32)], axis=0)


def apply(fac_ref, block, line, vec):
    out = []
    for i in range(V):
        out.append(
            dot([(fac_ref[block * 25 + i * V + k, line : line + 1, :], vec[k]) for k in range(V)])
        )
    return out


def condense(fac_ref, line, right, low, high):
    y0 = apply(fac_ref, 0, line, right(0))
    y1 = apply(fac_ref, 1, line, [r + l * y for r, l, y in zip(right(1), low(1), y0)])
    v2 = apply(fac_ref, 2, line, [r + l * y for r, l, y in zip(right(2), low(2), y1)])
    c1 = apply(fac_ref, 1, line, [h * v for h, v in zip(high(1), v2)])
    v1 = [p + q for p, q in zip(y1, c1)]
    c0 = apply(fac_ref, 0, line, [h * v for h, v in zip(high(0), v1)])
    v0 = [p + q for p, q in zip(y0, c0)]
    last = [r + l * v for r, l, v in zip(right(3), low(3), v2)]
    return v0, v1, v2, last


def spectral_terms(load, table, lanes_shape=(N, 128)):
    acc = [None] * V
    for k in range(N):
        t = table[k]
        for i in range(V):
            p = t * load(i, k)
            acc[i] = p if acc[i] is None else acc[i] + p
    return acc


def first_kernel(
    flag_ref, omega_ref, state_ref, source_ref, before_ref, after_ref, halo_ref, xf_ref, yf_ref,
    fac_ref, xmat_ref, spec_ref, r_ref, v_ref, msg_ref, table,
):
    flag = flag_ref[0]
    lanes = lane((N, 128))
    table[...] = spec_ref[...] * omega_ref[0]
    halo = halo_ref[...]
    for y in range(B):
        for x in range(B):
            spec = spectral_terms(lambda i, k: state_ref[x, y, i, k : k + 1, :], table)
            for i in range(V):
                s = state_ref[x, y, i]
                below = state_ref[x, y - 1, i] if y > 0 else before_ref[x, i]
                above = state_ref[x, y + 1, i] if y < B - 1 else after_ref[x, i]
                yl = yf_ref[0, x, y, i : i + 1, :]
                yh = yf_ref[1, x, y, i : i + 1, :]
                zn = z_neighbours(s, halo, (x * B + y) * V + i, flag, lanes)
                r = source_ref[x, y, i] - (yl + yh + 1.0) * s + yl * below + yh * above
                r_ref[x, y, i] = r + 0.5 * zn - spec[i]
    lanes8 = lane()
    for y in range(B):
        v0, v1, v2, last = condense(
            fac_ref, y,
            lambda t: [r_ref[t, y, i] for i in range(V)],
            lambda t: [xf_ref[0, t, y, i : i + 1, :] for i in range(V)],
            lambda t: [xf_ref[1, t, y, i : i + 1, :] for i in range(V)],
        )
        for i in range(V):
            v_ref[0, y, i] = v0[i]
            v_ref[1, y, i] = v1[i]
            v_ref[2, y, i] = v2[i]
            for ih, (e0, e1) in enumerate(zip(halves(last[i]), halves(v0[i]))):
                lo = jnp.where(lanes8 < 64, e0, swap(e1))
                hi = jnp.where(lanes8 < 64, swap(e0), e1)
                for zh, v in enumerate((lo, hi)):
                    msg_ref[y * 4 + zh * 2 + ih, i * H : (i + 1) * H, :] = v
    for d in range(16):
        msg_ref[d, 40:XR, :] = xmat_ref[d * MR : (d + 1) * MR, :]


def reduce_lines(a, b, c, r, shifted, steps, kk, nn, bi):
    for step in range(steps):
        inv = inverse([b[e] for e in range(25)])
        for e in range(25):
            bi[e] = inv[e]
        last = step == steps - 1
        for dst, src in ((kk, a), (nn, c)):
            m = [src[e] for e in range(25)]
            for i in range(V):
                row = [bi[i * V + k] for k in range(V)]
                for j in range(V):
                    dst[i * V + j] = dot([(row[k], m[k * V + j]) for k in range(V)])
        m = [shifted(nn[e], step, -1) for e in range(25)]
        for i in range(V):
            row = [a[i * V + k] for k in range(V)]
            for j in range(V):
                b[i * V + j] = b[i * V + j] - dot([(row[k], m[k * V + j]) for k in range(V)])
        m = [shifted(kk[e], step, 1) for e in range(25)]
        for i in range(V):
            row = [c[i * V + k] for k in range(V)]
            for j in range(V):
                b[i * V + j] = b[i * V + j] - dot([(row[k], m[k * V + j]) for k in range(V)])
        for n in range(H):
            old = [r[i * H + n] for i in range(V)]
            hat = [dot([(bi[i * V + k], old[k]) for k in range(V)]) for i in range(V)]
            before = [shifted(h, step, -1) for h in hat]
            after = [shifted(h, step, 1) for h in hat]
            for i in range(V):
                r[i * H + n] = (
                    old[i]
                    - dot([(a[i * V + k], before[k]) for k in range(V)])
                    - dot([(c[i * V + k], after[k]) for k in range(V)])
                )
        if not last:
            m = [shifted(kk[e], step, -1) for e in range(25)]
            for i in range(V):
                row = [a[i * V + k] for k in range(V)]
                for j in range(V):
                    a[i * V + j] = -dot([(row[k], m[k * V + j]) for k in range(V)])
            m = [shifted(nn[e], step, 1) for e in range(25)]
            for i in range(V):
                row = [c[i * V + k] for k in range(V)]
                for j in range(V):
                    c[i * V + j] = -dot([(row[k], m[k * V + j]) for k in range(V)])
    inv = inverse([b[e] for e in range(25)])
    for e in range(25):
        bi[e] = inv[e]
    for n in range(H):
        old = [r[i * H + n] for i in range(V)]
        for i in range(V):
            r[i * H + n] = dot([(bi[i * V + k], old[k]) for k in range(V)])


def close(b, c, r, fl, fh, first, edge, shift_after, edge_ok):
    for i in range(V):
        h = jnp.where(edge_ok, edge(i), 0.0)
        for j in range(V):
            e = i * V + j
            c[e] = -(h * shift_after(fh(e)))
            b[e] = b[e] - h * shift_after(fl(e))
        for n in range(H):
            r[i * H + n] = r[i * H + n] + h * shift_after(first(i, n))


def x_solver_kernel(msg_ref, out_ref, a, b, c, r, kk, nn, bi, fh, fl, first):
    lanes, subs = lane(), sub()
    left = lanes < 64

    def pair(row):
        p = msg_ref[pl.ds(row, 8, stride=XR), :]
        q = msg_ref[pl.ds(8 * XR + row, 8, stride=XR), :]
        return jnp.where(left, p, swap(q)), jnp.where(left, swap(p), q)

    def before(v, k):
        if k == 8:
            return swap(v)
        v = pltpu.roll(v, k, 0)
        return jnp.where(subs < k, swap(v), v)

    def after(v, k):
        if k == 8:
            return swap(v)
        v = pltpu.roll(v, 8 - k, 0)
        return jnp.where(subs >= 8 - k, swap(v), v)

    def shifted(v, step, sign):
        return before(v, 2**step) if sign < 0 else after(v, 2**step)

    begin = (subs == 0) & left
    end = (subs == 7) & (lanes >= 64)
    for e in range(25):
        low, fh[e] = pair(40 + e)
        a[e] = jnp.where(begin, 0.0, low)
        b[e], fl[e] = pair(65 + e)
    for e in range(40):
        r[e], first[e] = pair(e)
    close(
        b, c, r, lambda e: fl[e], lambda e: fh[e], lambda i, n: first[i * H + n],
        lambda i: pair(90 + i)[0], lambda v: after(v, 1), jnp.logical_not(end),
    )
    reduce_lines(a, b, c, r, shifted, 4, kk, nn, bi)
    for e in range(40):
        u = r[e]
        prev = jnp.where(begin, 0.0, before(u, 1))
        out_ref[pl.ds(e, 8, stride=40), :] = jnp.where(left, prev, swap(u))
        out_ref[pl.ds(320 + e, 8, stride=40), :] = jnp.where(left, swap(prev), u)


def y_solver_kernel(line_ref, msg_ref, mat_ref, out_ref, a, b, c, r, kk, nn, bi):
    subs = sub()

    def rhs(row):
        return msg_ref[pl.ds(row, 8, stride=YR), :]

    def mat(row):
        return mat_ref[:, 0, row, :]

    def before(v, k):
        return pltpu.roll(v, k, 0)

    def after(v, k):
        return pltpu.roll(v, 8 - k, 0)

    def shifted(v, step, sign):
        return before(v, 2**step) if sign < 0 else after(v, 2**step)

    begin = subs == 0
    for e in range(25):
        a[e] = jnp.where(begin, 0.0, mat(e))
        b[e] = mat(25 + e)
    for e in range(40):
        r[e] = rhs(e)
    close(
        b, c, r, lambda e: mat(50 + e), lambda e: mat(75 + e), lambda i, n: rhs(40 + i * H + n),
        lambda i: mat(100 + i), lambda v: after(v, 1), subs != 7,
    )
    reduce_lines(a, b, c, r, shifted, 3, kk, nn, bi)
    for e in range(40):
        u = r[e]
        out_ref[pl.ds(e, 8, stride=YR), :] = jnp.where(begin, 0.0, before(u, 1))
        out_ref[pl.ds(40 + e, 8, stride=YR), :] = u


def middle_kernel(flag_ref, ret_ref, v_ref, fac_ref, h_ref, edge_ref):
    left = lane() < 64
    for y in range(B):
        prev, cur = [], []
        for i in range(V):
            um, u = [], []
            for ih in range(2):
                z0 = ret_ref[y * 4 + ih, i * H : (i + 1) * H, :]
                z1 = ret_ref[y * 4 + 2 + ih, i * H : (i + 1) * H, :]
                um.append(jnp.where(left, z0, swap(z1)))
                u.append(jnp.where(left, swap(z0), z1))
            prev.append(jnp.concatenate(um, axis=0)[:N])
            cur.append(jnp.concatenate(u, axis=0)[:N])
        for t in range(B - 1):
            lo = apply(fac_ref, 3 + t, y, prev)
            hi = apply(fac_ref, 6 + t, y, cur)
            for i in range(V):
                h_ref[t, y, i] = v_ref[t, y, i] + lo[i] + hi[i]
        for i in range(V):
            h_ref[B - 1, y, i] = cur[i]
    edge_ref[...] = pack_edges(lambda x, y, i: h_ref[x, y, i], flag_ref[0])


def second_kernel(
    flag_ref, omega_ref, h_ref, source_ref, r_ref, halo_ref, couple_ref, yf_ref, fac_ref, spec_ref,
    v_ref, msg_ref, table, r2,
):
    flag = flag_ref[0]
    lanes = lane((N, 128))
    table[...] = spec_ref[...] * omega_ref[0]
    halo = halo_ref[...]
    for x in range(B):
        for y in range(B):
            spec = spectral_terms(lambda i, k: h_ref[x, y, i, k : k + 1, :], table)
            h = [h_ref[x, y, i] for i in range(V)]
            for i in range(V):
                zn = z_neighbours(h[i], halo, (x * B + y) * V + i, flag, lanes)
                c = dot([(couple_ref[x, y, i, k : k + 1, :], h[k]) for k in range(V)])
                r = source_ref[x, y, i] - r_ref[x, y, i] + c
                r2[x, y, i] = r - h[i] + 0.5 * zn - spec[i]
    for x in range(B):
        v0, v1, v2, last = condense(
            fac_ref, 4 + x,
            lambda t: [r2[x, t, i] for i in range(V)],
            lambda t: [yf_ref[0, x, t, i : i + 1, :] for i in range(V)],
            lambda t: [yf_ref[1, x, t, i : i + 1, :] for i in range(V)],
        )
        for i in range(V):
            v_ref[x, 0, i] = v0[i]
            v_ref[x, 1, i] = v1[i]
            v_ref[x, 2, i] = v2[i]
            for ih, (e0, e1) in enumerate(zip(halves(last[i]), halves(v0[i]))):
                msg_ref[x * 2 + ih, i * H : (i + 1) * H, :] = e0
                msg_ref[x * 2 + ih, 40 + i * H : 40 + (i + 1) * H, :] = e1


def last_kernel(ret_ref, v_ref, fac_ref, w_ref):
    for x in range(B):
        prev, cur = [], []
        for i in range(V):
            for out, at in ((prev, 0), (cur, 40)):
                rows = [
                    ret_ref[x * 2 + ih, at + i * H : at + (i + 1) * H, :] for ih in range(2)
                ]
                out.append(jnp.concatenate(rows, axis=0)[:N])
        for t in range(B - 1):
            lo = apply(fac_ref, 3 + t, 4 + x, prev)
            hi = apply(fac_ref, 6 + t, 4 + x, cur)
            for i in range(V):
                w_ref[x, t, i] = v_ref[x, t, i] + lo[i] + hi[i]
        for i in range(V):
            w_ref[x, B - 1, i] = cur[i]


smem = pl.BlockSpec(memory_space=pltpu.SMEM)
vmem = pl.BlockSpec(memory_space=pltpu.VMEM)


def sds(*shape):
    return jax.ShapeDtypeStruct(shape, f32)


def scratch(*shape):
    return pltpu.VMEM(shape, f32)


def call(kernel, ins, outs, scratches=(), **more):
    single = not isinstance(outs, (list, tuple))
    return pl.pallas_call(
        kernel,
        in_specs=list(ins),
        out_specs=vmem if single else [vmem] * len(outs),
        out_shape=outs,
        scratch_shapes=list(scratches),
        compiler_params=pltpu.CompilerParams(vmem_limit_bytes=40 * 2**20),
        **more,
    )


def body(state, source, x_faces, y_faces, couple, omega):
    n_y = lax.axis_size("gy")
    flag = lax.axis_index("gz").astype(jnp.int32).reshape(1)
    spec = jnp.asarray(spectral_columns())
    up = [(i, i + 1) for i in range(n_y - 1)]
    down = [(j, i) for i, j in up]
    flip = [(0, 1), (1, 0)]
    field = sds(B, B, V, N, 128)

    first, last, lanes = call(
        edge_kernel, [smem, vmem],
        [sds(B, V, N, 128), sds(B, V, N, 128), sds(N, 128)],
    )(flag, state)
    before = lax.ppermute(last, "gy", up)
    after = lax.ppermute(first, "gy", down)
    halo = lax.ppermute(lanes, "gz", flip)
    fac, xmat, ymat = call(
        matrix_kernel, [vmem] * 3,
        [sds(225, 8, 128), sds(16 * MR, 128), sds(B * YM, 128)],
        [scratch(B * 25 * 8, 128), scratch(B * V * 8, 128), scratch(B * V * 8, 128)],
    )(couple, x_faces, y_faces)
    all_mat = lax.all_gather(ymat, "gy").reshape(n_y, B, YM, 128)
    r1, v, msg = call(
        first_kernel, [smem, smem] + [vmem] * 10,
        [field, sds(B - 1, B, V, N, 128), sds(16, XR, 128)],
        [scratch(N, N, 128)],
    )(flag, omega, state, source, before, after, halo, x_faces, y_faces, fac, xmat, spec)
    got = lax.all_to_all(msg, "gx", 0, 0, tiled=True)
    mats = [scratch(25, 8, 128)] * 3 + [scratch(40, 8, 128)] + [scratch(25, 8, 128)] * 3
    ret = call(
        x_solver_kernel, [vmem], sds(16 * 40, 128),
        mats + [scratch(25, 8, 128), scratch(25, 8, 128), scratch(40, 8, 128)],
    )(got.reshape(16 * XR, 128))
    back = lax.all_to_all(ret.reshape(16, 40, 128), "gx", 0, 0, tiled=True)
    h, edge = call(
        middle_kernel, [smem, vmem, vmem, vmem], [field, sds(N, 128)]
    )(flag, back, v, fac)
    halo = lax.ppermute(edge, "gz", flip)
    v, msg = call(
        second_kernel, [smem, smem] + [vmem] * 8,
        [sds(B, B - 1, V, N, 128), sds(8, YR, 128)],
        [scratch(N, N, 128), scratch(B, B, V, N, 128)],
    )(flag, omega, h, source, r1, halo, couple, y_faces, fac, spec)
    got = lax.all_to_all(msg, "gy", 0, 0, tiled=True)
    line = (lax.axis_index("gy") // 2).astype(jnp.int32).reshape(1)
    ret = pl.pallas_call(
        y_solver_kernel,
        grid_spec=pltpu.PrefetchScalarGridSpec(
            num_scalar_prefetch=1,
            grid=(1,),
            in_specs=[
                pl.BlockSpec((8 * YR, 128), lambda i, line: (0, 0)),
                pl.BlockSpec((8, 1, YM, 128), lambda i, line: (0, line[0], 0, 0)),
            ],
            out_specs=pl.BlockSpec((8 * YR, 128), lambda i, line: (0, 0)),
            scratch_shapes=mats,
        ),
        out_shape=sds(8 * YR, 128),
        compiler_params=pltpu.CompilerParams(vmem_limit_bytes=40 * 2**20),
    )(line, got.reshape(8 * YR, 128), all_mat)
    back = lax.all_to_all(ret.reshape(8, YR, 128), "gy", 0, 0, tiled=True)
    return call(last_kernel, [vmem] * 3, field)(back, v, fac)


def solution(mesh):
    return jax.shard_map(
        body,
        mesh=mesh,
        in_specs=(
            P("gx", "gy", None, None, "gz"),
            P("gx", "gy", None, None, "gz"),
            P(None, "gx", "gy", None, "gz"),
            P(None, "gx", "gy", None, "gz"),
            P("gx", "gy", None, None, "gz"),
            P(),
        ),
        out_specs=P("gx", "gy", None, None, "gz"),
        check_vma=False,
    )
```

```python
import functools
import math

import jax
import jax.numpy as jnp
import numpy as np
from jax import lax
from jax.experimental import pallas as pl
from jax.experimental.pallas import tpu as pltpu
from jax.sharding import PartitionSpec as P


V = 5
N = 15
B = 4
H = 8
XR = 96
MR = 56
YR = 136
f32 = jnp.float32


def spectral_columns():
    offsets = np.arange(N)
    gaps = offsets[:, None] - offsets[None, :]
    signs = np.where(gaps % 2 == 0, 1.0, -1.0)
    sine = np.where(gaps == 0, 1.0, np.sin(math.pi * gaps / N))
    table = np.where(gaps == 0, 0.0, 0.5 * signs / sine).astype(np.float32)
    return np.ascontiguousarray(np.broadcast_to(table.T[:, :, None], (N, N, 128)))


def lane(shape=(8, 128)):
    return lax.broadcasted_iota(jnp.int32, shape, len(shape) - 1)


def sub(shape=(8, 128)):
    return lax.broadcasted_iota(jnp.int32, shape, len(shape) - 2)


def swap(v):
    return pltpu.roll(v, 64, 1)


def inverse(m):
    m = list(m)
    for p in range(V):
        piv = 1.0 / m[p * V + p]
        for j in range(V):
            if j != p:
                m[p * V + j] = m[p * V + j] * piv
        m[p * V + p] = piv
        for i in range(V):
            if i != p:
                f = m[i * V + p]
                for j in range(V):
                    if j != p:
                        m[i * V + j] = m[i * V + j] - f * m[p * V + j]
                m[i * V + p] = -f * piv
    return m


def dot(terms):
    total = None
    for a, b in terms:
        total = a * b if total is None else total + a * b
    return total


def matmul(a, b):
    return [
        dot([(a[i * V + k], b[k * V + j]) for k in range(V)]) for i in range(V) for j in range(V)
    ]


def pack_edges(load, flag):
    shift = jnp.where(flag == 0, 1, 0)
    lanes = lane((N, 128))
    acc = jnp.zeros((N, 128), f32)
    for c in range(B * B * V):
        x, y, i = c // (B * V), (c // V) % B, c % V
        acc = jnp.where(lanes == c, pltpu.roll(load(x, y, i), shift + c, 1), acc)
    return acc


def edge_kernel(flag_ref, state_ref, first_ref, last_ref, lanes_ref):
    first_ref[...] = state_ref[:, 0]
    last_ref[...] = state_ref[:, B - 1]
    lanes_ref[...] = pack_edges(lambda x, y, i: state_ref[x, y, i], flag_ref[0])


def z_neighbours(v, halo, c, flag, lanes):
    edge = jnp.where(flag == 0, 127, 0)
    low = jnp.where(lanes == 0, 0.0, pltpu.roll(v, 1, 1))
    high = jnp.where(lanes == 127, 0.0, pltpu.roll(v, 127, 1))
    shift = jnp.where(flag == 0, 127 - c, 128 - c)
    far = jnp.where(lanes == edge, pltpu.roll(halo, shift, 1), 0.0)
    return low + high + far


def matrix_kernel(couple_ref, xf_ref, yf_ref, fac_ref, xmat_ref, ymat_ref, mel, lo, hi):
    for a in range(B):
        for i in range(V):
            for j in range(V):
                c = couple_ref[a, i, j]
                e = i * V + j
                mel[(a * 25 + e) * 8 : (a * 25 + e) * 8 + 4, :] = c
                mel[pl.ds(e * 8 + 4 + a, B, stride=25 * 8), :] = c
            lo[(a * V + i) * 8 : (a * V + i) * 8 + 4, :] = xf_ref[0, a, i]
            hi[(a * V + i) * 8 : (a * V + i) * 8 + 4, :] = xf_ref[1, a, i]
            lo[pl.ds(i * 8 + 4 + a, B, stride=V * 8), :] = yf_ref[0, a, i]
            hi[pl.ds(i * 8 + 4 + a, B, stride=V * 8), :] = yf_ref[1, a, i]

    def row(ref, r):
        return ref[r * 8 : r * 8 + 8, :]

    low = [[row(lo, t * V + i) for i in range(V)] for t in range(B)]
    high = [[row(hi, t * V + i) for i in range(V)] for t in range(B)]

    def mid(t):
        m = [row(mel, t * 25 + e) for e in range(25)]
        for i in range(V):
            m[i * V + i] = m[i * V + i] + (low[t][i] + high[t][i])
        return m

    def put(block, m):
        for e in range(25):
            fac_ref[block * 25 + e] = m[e]

    def get(block):
        return [fac_ref[block * 25 + e] for e in range(25)]

    def rows_by(d, m):
        return [d[i] * m[i * V + j] for i in range(V) for j in range(V)]

    def cols_by(m, d):
        return [m[i * V + j] * d[j] for i in range(V) for j in range(V)]

    g0 = inverse(mid(0))
    put(0, g0)
    m1 = mid(1)
    s = rows_by(low[1], cols_by(g0, high[0]))
    g1 = inverse([p - q for p, q in zip(m1, s)])
    put(1, g1)
    m2 = mid(2)
    s = rows_by(low[2], cols_by(g1, high[1]))
    g2 = inverse([p - q for p, q in zip(m2, s)])
    put(2, g2)
    e2 = cols_by(g2, high[2])
    put(8, e2)
    e1 = matmul(get(1), rows_by(high[1], e2))
    put(7, e1)
    e0 = matmul(get(0), rows_by(high[0], e1))
    put(6, e0)
    l0 = cols_by(get(0), low[0])
    l1 = matmul(get(1), rows_by(low[1], l0))
    l2 = matmul(get(2), rows_by(low[2], l1))
    put(5, l2)
    b1 = matmul(get(1), rows_by(high[1], l2))
    l1 = [p + q for p, q in zip(l1, b1)]
    put(4, l1)
    b0 = matmul(get(0), rows_by(high[0], l1))
    l0 = [p + q for p, q in zip(cols_by(get(0), low[0]), b0)]
    put(3, l0)

    lanes = lane()
    m3 = mid(3)
    last_low, last_high = get(5), get(8)
    first_low, first_high = get(3), get(6)

    def put_pair(r, e0, e1):
        for zh in range(2):
            if zh == 0:
                v = jnp.where(lanes < 64, e0, swap(e1))
            else:
                v = jnp.where(lanes < 64, swap(e0), e1)
            for ih in range(2):
                xmat_ref[pl.ds((zh * 2 + ih) * MR + r, 4, stride=4 * MR), :] = v[0:4]
            ymat_ref[pl.ds(zh * MR + r, 4, stride=2 * MR), :] = v[4:8]

    for i in range(V):
        for j in range(V):
            e = i * V + j
            put_pair(e, -(low[3][i] * last_low[e]), first_high[e])
            put_pair(25 + e, m3[e] - low[3][i] * last_high[e], first_low[e])
    zero = jnp.zeros((8, 128), f32)
    put_pair(50, high[3][0], high[3][1])
    put_pair(51, high[3][2], high[3][3])
    put_pair(52, high[3][4], zero)
    for r in range(53, MR):
        put_pair(r, zero, zero)


def halves(v):
    return v[0:H], jnp.concatenate([v[H:N], jnp.zeros((1, 128), f32)], axis=0)


def apply(fac_ref, block, line, vec):
    out = []
    for i in range(V):
        out.append(
            dot([(fac_ref[block * 25 + i * V + k, line : line + 1, :], vec[k]) for k in range(V)])
        )
    return out


def condense(fac_ref, line, right, low, high):
    y0 = apply(fac_ref, 0, line, right(0))
    y1 = apply(fac_ref, 1, line, [r + l * y for r, l, y in zip(right(1), low(1), y0)])
    v2 = apply(fac_ref, 2, line, [r + l * y for r, l, y in zip(right(2), low(2), y1)])
    c1 = apply(fac_ref, 1, line, [h * v for h, v in zip(high(1), v2)])
    v1 = [p + q for p, q in zip(y1, c1)]
    c0 = apply(fac_ref, 0, line, [h * v for h, v in zip(high(0), v1)])
    v0 = [p + q for p, q in zip(y0, c0)]
    last = [r + l * v for r, l, v in zip(right(3), low(3), v2)]
    return v0, v1, v2, last


def spectral_terms(load, table, lanes_shape=(N, 128)):
    acc = [None] * V
    for k in range(N):
        t = table[k]
        for i in range(V):
            p = t * load(i, k)
            acc[i] = p if acc[i] is None else acc[i] + p
    return acc


def first_kernel(
    flag_ref, omega_ref, state_ref, source_ref, before_ref, after_ref, halo_ref, xf_ref, yf_ref,
    fac_ref, xmat_ref, spec_ref, r_ref, v_ref, msg_ref, table,
):
    flag = flag_ref[0]
    lanes = lane((N, 128))
    table[...] = spec_ref[...] * omega_ref[0]
    halo = halo_ref[...]
    for y in range(B):
        for x in range(B):
            spec = spectral_terms(lambda i, k: state_ref[x, y, i, k : k + 1, :], table)
            for i in range(V):
                s = state_ref[x, y, i]
                below = state_ref[x, y - 1, i] if y > 0 else before_ref[x, i]
                above = state_ref[x, y + 1, i] if y < B - 1 else after_ref[x, i]
                yl = yf_ref[0, x, i, y : y + 1, :]
                yh = yf_ref[1, x, i, y : y + 1, :]
                zn = z_neighbours(s, halo, (x * B + y) * V + i, flag, lanes)
                r = source_ref[x, y, i] - (yl + yh + 1.0) * s + yl * below + yh * above
                r_ref[x, y, i] = r + 0.5 * zn - spec[i]
    lanes8 = lane()
    for y in range(B):
        v0, v1, v2, last = condense(
            fac_ref, y,
            lambda t: [r_ref[t, y, i] for i in range(V)],
            lambda t: [xf_ref[0, t, i, y : y + 1, :] for i in range(V)],
            lambda t: [xf_ref[1, t, i, y : y + 1, :] for i in range(V)],
        )
        for i in range(V):
            v_ref[0, y, i] = v0[i]
            v_ref[1, y, i] = v1[i]
            v_ref[2, y, i] = v2[i]
            for ih, (e0, e1) in enumerate(zip(halves(last[i]), halves(v0[i]))):
                lo = jnp.where(lanes8 < 64, e0, swap(e1))
                hi = jnp.where(lanes8 < 64, swap(e0), e1)
                for zh, v in enumerate((lo, hi)):
                    msg_ref[y * 4 + zh * 2 + ih, i * H : (i + 1) * H, :] = v
    for d in range(16):
        msg_ref[d, 40:XR, :] = xmat_ref[d * MR : (d + 1) * MR, :]


def minus_product(out, a, m, keep=True):
    for i in range(V):
        row = [a[i * V + k] for k in range(V)]
        for j in range(V):
            p = dot([(row[k], m[k * V + j]) for k in range(V)])
            out[i * V + j] = out[i * V + j] - p if keep else -p


def left_apply(inv, src, dst):
    m = [src[e] for e in range(25)]
    for i in range(V):
        row = [inv[i * V + k] for k in range(V)]
        for j in range(V):
            dst[i * V + j] = dot([(row[k], m[k * V + j]) for k in range(V)])


def reduce_lines(a, b, c, r, shifted, steps, kk, nn, bi, lower):
    def invert():
        inv = inverse([b[e] for e in range(25)])
        for e in range(25):
            bi[e] = inv[e]

    for step in range(steps - 1):
        invert()
        left_apply(bi, a, kk)
        left_apply(bi, c, nn)
        for n in range(H):
            old = [r[i * H + n] for i in range(V)]
            hat = [dot([(bi[i * V + k], old[k]) for k in range(V)]) for i in range(V)]
            before = [shifted(h, step, -1) for h in hat]
            after = [shifted(h, step, 1) for h in hat]
            for i in range(V):
                r[i * H + n] = (
                    old[i]
                    - dot([(a[i * V + k], before[k]) for k in range(V)])
                    - dot([(c[i * V + k], after[k]) for k in range(V)])
                )
        minus_product(b, a, [shifted(nn[e], step, -1) for e in range(25)])
        minus_product(b, c, [shifted(kk[e], step, 1) for e in range(25)])
        minus_product(a, a, [shifted(kk[e], step, -1) for e in range(25)], keep=False)
        minus_product(c, c, [shifted(nn[e], step, 1) for e in range(25)], keep=False)
    invert()
    for e in range(25):
        a[e] = jnp.where(lower, c[e], a[e])
    left_apply(bi, a, kk)
    for n in range(H):
        old = [r[i * H + n] for i in range(V)]
        hat = [dot([(bi[i * V + k], old[k]) for k in range(V)]) for i in range(V)]
        far = [shifted(h, steps - 1, 1) for h in hat]
        for i in range(V):
            r[i * H + n] = old[i] - dot([(a[i * V + k], far[k]) for k in range(V)])
    minus_product(b, a, [shifted(kk[e], steps - 1, 1) for e in range(25)])
    invert()
    for n in range(H):
        old = [r[i * H + n] for i in range(V)]
        for i in range(V):
            r[i * H + n] = dot([(bi[i * V + k], old[k]) for k in range(V)])


def close(b, c, r, fl, fh, first, edge, shift_after, edge_ok):
    for i in range(V):
        h = jnp.where(edge_ok, edge(i), 0.0)
        for j in range(V):
            e = i * V + j
            c[e] = -(h * shift_after(fh(e)))
            b[e] = b[e] - h * shift_after(fl(e))
        for n in range(H):
            r[i * H + n] = r[i * H + n] + h * shift_after(first(i, n))


def x_solver_kernel(msg_ref, out_ref, a, b, c, r, kk, nn, bi, fh, fl, first):
    lanes, subs = lane(), sub()
    left = lanes < 64

    def pair(row):
        p = msg_ref[pl.ds(row, 8, stride=XR), :]
        q = msg_ref[pl.ds(8 * XR + row, 8, stride=XR), :]
        return jnp.where(left, p, swap(q)), jnp.where(left, swap(p), q)

    def before(v, k):
        if k == 8:
            return swap(v)
        v = pltpu.roll(v, k, 0)
        return jnp.where(subs < k, swap(v), v)

    def after(v, k):
        if k == 8:
            return swap(v)
        v = pltpu.roll(v, 8 - k, 0)
        return jnp.where(subs >= 8 - k, swap(v), v)

    def shifted(v, step, sign):
        return before(v, 2**step) if sign < 0 else after(v, 2**step)

    begin = (subs == 0) & left
    end = (subs == 7) & (lanes >= 64)
    for e in range(25):
        low, fh[e] = pair(40 + e)
        a[e] = jnp.where(begin, 0.0, low)
        b[e], fl[e] = pair(65 + e)
    for e in range(40):
        r[e], first[e] = pair(e)
    close(
        b, c, r, lambda e: fl[e], lambda e: fh[e], lambda i, n: first[i * H + n],
        lambda i: pair(90 + i // 2)[i % 2], lambda v: after(v, 1), jnp.logical_not(end),
    )
    reduce_lines(a, b, c, r, shifted, 4, kk, nn, bi, left)
    for e in range(40):
        u = r[e]
        prev = jnp.where(begin, 0.0, before(u, 1))
        out_ref[pl.ds(e, 8, stride=40), :] = jnp.where(left, prev, swap(u))
        out_ref[pl.ds(320 + e, 8, stride=40), :] = jnp.where(left, swap(prev), u)


def y_solver_kernel(msg_ref, out_ref, a, b, c, r, kk, nn, bi, fh, fl):
    lanes, subs = lane(), sub()
    left = lanes < 64

    def rhs(row):
        return msg_ref[pl.ds(row, 8, stride=YR), :]

    def pair(row):
        p = rhs(row)
        q = swap(p)
        return jnp.where(left, p, q), jnp.where(left, q, p)

    def before(v, k):
        return pltpu.roll(v, k, 0)

    def after(v, k):
        return pltpu.roll(v, 8 - k, 0)

    def shifted(v, step, sign):
        return before(v, 2**step) if sign < 0 else after(v, 2**step)

    begin = subs == 0
    for e in range(25):
        low, fh[e] = pair(80 + e)
        a[e] = jnp.where(begin, 0.0, low)
        b[e], fl[e] = pair(105 + e)
    for e in range(40):
        r[e] = rhs(e)
    close(
        b, c, r, lambda e: fl[e], lambda e: fh[e], lambda i, n: rhs(40 + i * H + n),
        lambda i: pair(130 + i // 2)[i % 2], lambda v: after(v, 1), subs != 7,
    )
    reduce_lines(a, b, c, r, shifted, 3, kk, nn, bi, subs < 4)
    for e in range(40):
        u = r[e]
        out_ref[pl.ds(e, 8, stride=80), :] = jnp.where(begin, 0.0, before(u, 1))
        out_ref[pl.ds(40 + e, 8, stride=80), :] = u


def middle_kernel(flag_ref, ret_ref, v_ref, fac_ref, h_ref, edge_ref):
    left = lane() < 64
    for y in range(B):
        prev, cur = [], []
        for i in range(V):
            um, u = [], []
            for ih in range(2):
                z0 = ret_ref[y * 4 + ih, i * H : (i + 1) * H, :]
                z1 = ret_ref[y * 4 + 2 + ih, i * H : (i + 1) * H, :]
                um.append(jnp.where(left, z0, swap(z1)))
                u.append(jnp.where(left, swap(z0), z1))
            prev.append(jnp.concatenate(um, axis=0)[:N])
            cur.append(jnp.concatenate(u, axis=0)[:N])
        for t in range(B - 1):
            lo = apply(fac_ref, 3 + t, y, prev)
            hi = apply(fac_ref, 6 + t, y, cur)
            for i in range(V):
                h_ref[t, y, i] = v_ref[t, y, i] + lo[i] + hi[i]
        for i in range(V):
            h_ref[B - 1, y, i] = cur[i]
    edge_ref[...] = pack_edges(lambda x, y, i: h_ref[x, y, i], flag_ref[0])


def second_kernel(
    flag_ref, omega_ref, h_ref, source_ref, r_ref, halo_ref, couple_ref, yf_ref, fac_ref, ymat_ref,
    spec_ref, v_ref, msg_ref, table, r2,
):
    flag = flag_ref[0]
    lanes = lane((N, 128))
    table[...] = spec_ref[...] * omega_ref[0]
    halo = halo_ref[...]
    for x in range(B):
        for y in range(B):
            spec = spectral_terms(lambda i, k: h_ref[x, y, i, k : k + 1, :], table)
            h = [h_ref[x, y, i] for i in range(V)]
            for i in range(V):
                zn = z_neighbours(h[i], halo, (x * B + y) * V + i, flag, lanes)
                c = dot([(couple_ref[x, i, k, y : y + 1, :], h[k]) for k in range(V)])
                r = source_ref[x, y, i] - r_ref[x, y, i] + c
                r2[x, y, i] = r - h[i] + 0.5 * zn - spec[i]
    left = lane() < 64
    for x in range(B):
        v0, v1, v2, last = condense(
            fac_ref, 4 + x,
            lambda t: [r2[x, t, i] for i in range(V)],
            lambda t: [yf_ref[0, x, i, t : t + 1, :] for i in range(V)],
            lambda t: [yf_ref[1, x, i, t : t + 1, :] for i in range(V)],
        )
        for i in range(V):
            v_ref[x, 0, i] = v0[i]
            v_ref[x, 1, i] = v1[i]
            v_ref[x, 2, i] = v2[i]
            for at, v in ((0, last[i]), (40, v0[i])):
                e0, e1 = halves(v)
                rows = slice(at + i * H, at + (i + 1) * H)
                msg_ref[x * 2, rows, :] = jnp.where(left, e0, swap(e1))
                msg_ref[x * 2 + 1, rows, :] = jnp.where(left, swap(e0), e1)
    for d in range(8):
        msg_ref[d, 80:YR, :] = ymat_ref[d * MR : (d + 1) * MR, :]


def last_kernel(ret_ref, v_ref, fac_ref, w_ref):
    left = lane() < 64

    def put(x, y, i, v):
        w_ref[pl.ds((x * V + i) * N * B + y, N, stride=B), :] = v

    for x in range(B):
        prev, cur = [], []
        for i in range(V):
            for out, at in ((prev, 0), (cur, 40)):
                z0 = ret_ref[x * 2, at + i * H : at + (i + 1) * H, :]
                z1 = ret_ref[x * 2 + 1, at + i * H : at + (i + 1) * H, :]
                rows = [jnp.where(left, z0, swap(z1)), jnp.where(left, swap(z0), z1)]
                out.append(jnp.concatenate(rows, axis=0)[:N])
        for t in range(B - 1):
            lo = apply(fac_ref, 3 + t, 4 + x, prev)
            hi = apply(fac_ref, 6 + t, 4 + x, cur)
            for i in range(V):
                put(x, t, i, v_ref[x, t, i] + lo[i] + hi[i])
        for i in range(V):
            put(x, B - 1, i, cur[i])


smem = pl.BlockSpec(memory_space=pltpu.SMEM)
vmem = pl.BlockSpec(memory_space=pltpu.VMEM)


def sds(*shape):
    return jax.ShapeDtypeStruct(shape, f32)


def scratch(*shape):
    return pltpu.VMEM(shape, f32)


def call(kernel, ins, outs, scratches=(), **more):
    single = not isinstance(outs, (list, tuple))
    return pl.pallas_call(
        kernel,
        in_specs=list(ins),
        out_specs=vmem if single else [vmem] * len(outs),
        out_shape=outs,
        scratch_shapes=list(scratches),
        compiler_params=pltpu.CompilerParams(vmem_limit_bytes=40 * 2**20),
        **more,
    )


def body(state, source, x_faces, y_faces, couple, omega):
    n_y = lax.axis_size("gy")
    flag = lax.axis_index("gz").astype(jnp.int32).reshape(1)
    spec = jnp.asarray(spectral_columns())
    up = [(i, i + 1) for i in range(n_y - 1)]
    down = [(j, i) for i, j in up]
    flip = [(0, 1), (1, 0)]
    field = sds(B, B, V, N, 128)

    first, last, lanes = call(
        edge_kernel, [smem, vmem],
        [sds(B, V, N, 128), sds(B, V, N, 128), sds(N, 128)],
    )(flag, state)
    before = lax.ppermute(last, "gy", up)
    after = lax.ppermute(first, "gy", down)
    halo = lax.ppermute(lanes, "gz", flip)
    couple = jnp.transpose(couple, (0, 2, 3, 1, 4))
    x_faces = jnp.transpose(x_faces, (0, 1, 3, 2, 4))
    y_faces = jnp.transpose(y_faces, (0, 1, 3, 2, 4))
    fac, xmat, ymat = call(
        matrix_kernel, [vmem] * 3,
        [sds(225, 8, 128), sds(16 * MR, 128), sds(8 * MR, 128)],
        [scratch(B * 25 * 8, 128), scratch(B * V * 8, 128), scratch(B * V * 8, 128)],
        cost_estimate=pl.CostEstimate(flops=10**8, bytes_accessed=4 * 10**6, transcendentals=0),
    )(couple, x_faces, y_faces)
    r1, v, msg = call(
        first_kernel, [smem, smem] + [vmem] * 10,
        [field, sds(B - 1, B, V, N, 128), sds(16, XR, 128)],
        [scratch(N, N, 128)],
    )(flag, omega, state, source, before, after, halo, x_faces, y_faces, fac, xmat, spec)
    got = lax.all_to_all(msg, "gx", 0, 0, tiled=True)
    mats = [scratch(25, 8, 128)] * 3 + [scratch(40, 8, 128)] + [scratch(25, 8, 128)] * 3
    ret = call(
        x_solver_kernel, [vmem], sds(16 * 40, 128),
        mats + [scratch(25, 8, 128), scratch(25, 8, 128), scratch(40, 8, 128)],
    )(got.reshape(16 * XR, 128))
    back = lax.all_to_all(ret.reshape(16, 40, 128), "gx", 0, 0, tiled=True)
    h, edge = call(
        middle_kernel, [smem, vmem, vmem, vmem], [field, sds(N, 128)]
    )(flag, back, v, fac)
    halo = lax.ppermute(edge, "gz", flip)
    v, msg = call(
        second_kernel, [smem, smem] + [vmem] * 9,
        [sds(B, B - 1, V, N, 128), sds(8, YR, 128)],
        [scratch(N, N, 128), scratch(B, B, V, N, 128)],
    )(flag, omega, h, source, r1, halo, couple, y_faces, fac, ymat, spec)
    got = lax.all_to_all(msg, "gy", 0, 0, tiled=True)
    ret = call(
        y_solver_kernel, [vmem], sds(8 * 80, 128),
        mats + [scratch(25, 8, 128), scratch(25, 8, 128)],
    )(got.reshape(8 * YR, 128))
    back = lax.all_to_all(ret.reshape(8, 80, 128), "gy", 0, 0, tiled=True)
    out = call(last_kernel, [vmem] * 3, sds(B * V * N * B, 128))(back, v, fac)
    return jnp.transpose(out.reshape(B, V, N, B, 128), (0, 3, 1, 2, 4))


def solution(mesh):
    return jax.shard_map(
        body,
        mesh=mesh,
        in_specs=(
            P("gx", "gy", None, None, "gz"),
            P("gx", "gy", None, None, "gz"),
            P(None, "gx", "gy", None, "gz"),
            P(None, "gx", "gy", None, "gz"),
            P("gx", "gy", None, None, "gz"),
            P(),
        ),
        out_specs=P("gx", "gy", None, None, "gz"),
        check_vma=False,
    )
```

```python
import functools
import math

import jax
import jax.numpy as jnp
import numpy as np
from jax import lax
from jax.experimental import pallas as pl
from jax.experimental.pallas import tpu as pltpu
from jax.sharding import PartitionSpec as P


V = 5
N = 15
B = 4
H = 8
XR = 96
MR = 56
YR = 136
LINE = B * V * N * B
f32 = jnp.float32


def spectral_columns():
    offsets = np.arange(N)
    gaps = offsets[:, None] - offsets[None, :]
    signs = np.where(gaps % 2 == 0, 1.0, -1.0)
    sine = np.where(gaps == 0, 1.0, np.sin(math.pi * gaps / N))
    table = np.where(gaps == 0, 0.0, 0.5 * signs / sine).astype(np.float32)
    return np.ascontiguousarray(np.broadcast_to(table.T[:, :, None], (N, N, 128)))


def lane(shape=(8, 128)):
    return lax.broadcasted_iota(jnp.int32, shape, len(shape) - 1)


def sub(shape=(8, 128)):
    return lax.broadcasted_iota(jnp.int32, shape, len(shape) - 2)


def swap(v):
    return pltpu.roll(v, 64, 1)


def split(e0, e1):
    far, left = swap(e1), lane() < 64
    return jnp.where(left, e0, far), jnp.where(left, far, e0)


def join(z0, z1):
    left = lane() < 64
    return jnp.where(left, z0, z1), swap(jnp.where(left, z1, z0))


def choose(flag, p, q):
    return jnp.where(flag, q, p), jnp.where(flag, p, q)


def inverse(m):
    m = list(m)
    for p in range(V):
        piv = 1.0 / m[p * V + p]
        for j in range(V):
            if j != p:
                m[p * V + j] = m[p * V + j] * piv
        m[p * V + p] = piv
        for i in range(V):
            if i != p:
                f = m[i * V + p]
                for j in range(V):
                    if j != p:
                        m[i * V + j] = m[i * V + j] - f * m[p * V + j]
                m[i * V + p] = -f * piv
    return m


def dot(terms):
    total = None
    for a, b in terms:
        total = a * b if total is None else total + a * b
    return total


def matmul(a, b):
    return [
        dot([(a[i * V + k], b[k * V + j]) for k in range(V)]) for i in range(V) for j in range(V)
    ]


def edge_kernel(flag_ref, state_ref, near_ref, far_ref):
    even = flag_ref[1] == 0
    for x in range(B):
        for i in range(V):
            at = (x * V + i) * N * B
            first = state_ref[pl.ds(at, N, stride=B), :]
            last = state_ref[pl.ds(at + B - 1, N, stride=B), :]
            near_ref[x, i], far_ref[x, i] = choose(even, first, last)


def pack_edges(load, flag):
    shift = jnp.where(flag == 0, 1, 0)
    lanes = lane((N, 128))
    acc = jnp.zeros((N, 128), f32)
    for c in range(B * B * V):
        x, y, i = c // (B * V), (c // V) % B, c % V
        acc = jnp.where(lanes == c, pltpu.roll(load(x, y, i), shift + c, 1), acc)
    return acc


def z_inner(v, lanes):
    low = jnp.where(lanes == 0, 0.0, pltpu.roll(v, 1, 1))
    high = jnp.where(lanes == 127, 0.0, pltpu.roll(v, 127, 1))
    return low + high


def z_outer(halo, c, flag, lanes):
    edge = jnp.where(flag == 0, 127, 0)
    shift = jnp.where(flag == 0, 127 - c, 128 - c)
    return jnp.where(lanes == edge, pltpu.roll(halo, shift, 1), 0.0)


def matrix_kernel(
    flag_ref, state_ref, couple_ref, xf_ref, yf_ref, fac_ref, xmat_ref, ymat_ref, edge_ref, mel, lo, hi
):
    edge_ref[...] = pack_edges(lambda x, y, i: state_ref[x, y, i], flag_ref[0])
    for a in range(B):
        for i in range(V):
            for j in range(V):
                c = couple_ref[a, i, j]
                e = i * V + j
                mel[(a * 25 + e) * 8 : (a * 25 + e) * 8 + 4, :] = c
                mel[pl.ds(e * 8 + 4 + a, B, stride=25 * 8), :] = c
            lo[(a * V + i) * 8 : (a * V + i) * 8 + 4, :] = xf_ref[0, a, i]
            hi[(a * V + i) * 8 : (a * V + i) * 8 + 4, :] = xf_ref[1, a, i]
            lo[pl.ds(i * 8 + 4 + a, B, stride=V * 8), :] = yf_ref[0, a, i]
            hi[pl.ds(i * 8 + 4 + a, B, stride=V * 8), :] = yf_ref[1, a, i]

    def row(ref, r):
        return ref[r * 8 : r * 8 + 8, :]

    low = [[row(lo, t * V + i) for i in range(V)] for t in range(B)]
    high = [[row(hi, t * V + i) for i in range(V)] for t in range(B)]

    def mid(t):
        m = [row(mel, t * 25 + e) for e in range(25)]
        for i in range(V):
            m[i * V + i] = m[i * V + i] + (low[t][i] + high[t][i])
        return m

    def put(block, m):
        for e in range(25):
            fac_ref[block * 25 + e] = m[e]

    def get(block):
        return [fac_ref[block * 25 + e] for e in range(25)]

    def rows_by(d, m):
        return [d[i] * m[i * V + j] for i in range(V) for j in range(V)]

    def cols_by(m, d):
        return [m[i * V + j] * d[j] for i in range(V) for j in range(V)]

    g0 = inverse(mid(0))
    put(0, g0)
    m1 = mid(1)
    s = rows_by(low[1], cols_by(g0, high[0]))
    g1 = inverse([p - q for p, q in zip(m1, s)])
    put(1, g1)
    m2 = mid(2)
    s = rows_by(low[2], cols_by(g1, high[1]))
    g2 = inverse([p - q for p, q in zip(m2, s)])
    put(2, g2)
    e2 = cols_by(g2, high[2])
    put(8, e2)
    e1 = matmul(get(1), rows_by(high[1], e2))
    put(7, e1)
    e0 = matmul(get(0), rows_by(high[0], e1))
    put(6, e0)
    l0 = cols_by(get(0), low[0])
    l1 = matmul(get(1), rows_by(low[1], l0))
    l2 = matmul(get(2), rows_by(low[2], l1))
    put(5, l2)
    b1 = matmul(get(1), rows_by(high[1], l2))
    l1 = [p + q for p, q in zip(l1, b1)]
    put(4, l1)
    b0 = matmul(get(0), rows_by(high[0], l1))
    l0 = [p + q for p, q in zip(cols_by(get(0), low[0]), b0)]
    put(3, l0)

    lanes = lane()
    m3 = mid(3)
    last_low, last_high = get(5), get(8)
    first_low, first_high = get(3), get(6)

    blocks = [[], [], [], []]
    for i in range(V):
        for j in range(V):
            e = i * V + j
            blocks[0].append(-(low[3][i] * last_low[e]))
            blocks[1].append(m3[e] - low[3][i] * last_high[e])
            blocks[2].append(first_low[e])
            blocks[3].append(first_high[e])
    zero = jnp.zeros((8, 128), f32)
    edge = [high[3][i] for i in range(V)]
    odd = flag_ref[4] == 1
    for r in range(55):
        if r < 50:
            e0, e1 = blocks[0 if r < 25 else 1][r % 25], blocks[3 if r < 25 else 2][r % 25]
        else:
            e0, e1 = edge[r - 50], zero
        for zh, v in enumerate(split(*choose(odd, e0, e1))):
            for ih in range(2):
                xmat_ref[pl.ds((zh * 2 + ih) * MR + r, 4, stride=4 * MR), :] = v[0:4]
        for zh, v in enumerate(split(e0, e1)):
            ymat_ref[pl.ds(zh * MR + r, 4, stride=2 * MR), :] = v[4:8]
    for d in range(16):
        xmat_ref[d * MR + 55 : (d + 1) * MR, :] = jnp.zeros((1, 128), f32)
    for d in range(8):
        ymat_ref[d * MR + 55 : (d + 1) * MR, :] = jnp.zeros((1, 128), f32)


def halves(v):
    return v[0:H], jnp.concatenate([v[H:N], jnp.zeros((1, 128), f32)], axis=0)


def apply(fac_ref, block, line, vec):
    out = []
    for i in range(V):
        out.append(
            dot([(fac_ref[block * 25 + i * V + k, line : line + 1, :], vec[k]) for k in range(V)])
        )
    return out


def condense(fac_ref, line, right, low, high):
    y0 = apply(fac_ref, 0, line, right(0))
    y1 = apply(fac_ref, 1, line, [r + l * y for r, l, y in zip(right(1), low(1), y0)])
    v2 = apply(fac_ref, 2, line, [r + l * y for r, l, y in zip(right(2), low(2), y1)])
    c1 = apply(fac_ref, 1, line, [h * v for h, v in zip(high(1), v2)])
    v1 = [p + q for p, q in zip(y1, c1)]
    c0 = apply(fac_ref, 0, line, [h * v for h, v in zip(high(0), v1)])
    v0 = [p + q for p, q in zip(y0, c0)]
    last = [r + l * v for r, l, v in zip(right(3), low(3), v2)]
    return v0, v1, v2, last


def spectral_terms(load, table, lanes_shape=(N, 128)):
    acc = [None] * V
    for k in range(N):
        t = table[k]
        for i in range(V):
            p = t * load(i, k)
            acc[i] = p if acc[i] is None else acc[i] + p
    return acc


def scaled_table(spec_ref, omega_ref, table):
    table[...] = spec_ref[...] * omega_ref[0]


def inner_kernel(omega_ref, state_ref, source_ref, yf_ref, spec_ref, r_ref, table):
    lanes = lane((N, 128))
    scaled_table(spec_ref, omega_ref, table)
    for y in range(B):
        for x in range(B):
            spec = spectral_terms(lambda i, k: state_ref[x, y, i, k : k + 1, :], table)
            for i in range(V):
                s = state_ref[x, y, i]
                yl = yf_ref[0, x, i, y : y + 1, :]
                yh = yf_ref[1, x, i, y : y + 1, :]
                r = source_ref[x, y, i] - (yl + yh + 1.0) * s + 0.5 * z_inner(s, lanes)
                if y > 0:
                    r = r + yl * state_ref[x, y - 1, i]
                if y < B - 1:
                    r = r + yh * state_ref[x, y + 1, i]
                r_ref[x, y, i] = r - spec[i]


def first_kernel(
    flag_ref, part_ref, near_ref, far_ref, halo_ref, xf_ref, yf_ref, fac_ref, xmat_ref,
    r_ref, v_ref, msg_ref,
):
    flag = flag_ref[0]
    lanes = lane((N, 128))
    halo = halo_ref[...]
    even, begin, end = flag_ref[1] == 0, flag_ref[2] == 0, flag_ref[2] == flag_ref[3] - 1
    odd = flag_ref[4] == 1
    for y in range(B):
        for x in range(B):
            for i in range(V):
                r = part_ref[x, y, i] + 0.5 * z_outer(halo, (x * B + y) * V + i, flag, lanes)
                if y == 0:
                    below = jnp.where(even, far_ref[x, i], near_ref[x, i])
                    r = r + yf_ref[0, x, i, y : y + 1, :] * jnp.where(begin, 0.0, below)
                if y == B - 1:
                    above = jnp.where(even, near_ref[x, i], far_ref[x, i])
                    r = r + yf_ref[1, x, i, y : y + 1, :] * jnp.where(end, 0.0, above)
                r_ref[x, y, i] = r
    for y in range(B):
        v0, v1, v2, last = condense(
            fac_ref, y,
            lambda t: [r_ref[t, y, i] for i in range(V)],
            lambda t: [xf_ref[0, t, i, y : y + 1, :] for i in range(V)],
            lambda t: [xf_ref[1, t, i, y : y + 1, :] for i in range(V)],
        )
        for i in range(V):
            v_ref[0, y, i] = v0[i]
            v_ref[1, y, i] = v1[i]
            v_ref[2, y, i] = v2[i]
            for ih, (e0, e1) in enumerate(zip(halves(last[i]), halves(v0[i]))):
                for zh, v in enumerate(split(*choose(odd, e0, e1))):
                    msg_ref[y * 4 + zh * 2 + ih, i * H : (i + 1) * H, :] = v
    for d in range(16):
        msg_ref[d, 40:XR, :] = xmat_ref[d * MR : (d + 1) * MR, :]


def minus_product(out, a, m, keep=True, into=None):
    into = out if into is None else into
    for i in range(V):
        row = [a[i * V + k] for k in range(V)]
        for j in range(V):
            p = dot([(row[k], m[k * V + j]) for k in range(V)])
            into[i * V + j] = out[i * V + j] - p if keep else -p


def left_apply(inv, src, dst):
    m = [src[e] for e in range(25)]
    for i in range(V):
        row = [inv[i * V + k] for k in range(V)]
        for j in range(V):
            dst[i * V + j] = dot([(row[k], m[k * V + j]) for k in range(V)])


def reduce_lines(a, b, c, r, around, far, steps, kk, nn, bi, lower):
    def invert():
        inv = inverse([b[e] for e in range(25)])
        for e in range(25):
            bi[e] = inv[e]

    for step in range(steps - 1):
        k = 2**step
        invert()
        left_apply(bi, a, kk)
        left_apply(bi, c, nn)
        for n in range(H):
            old = [r[i * H + n] for i in range(V)]
            hat = [dot([(bi[i * V + q], old[q]) for q in range(V)]) for i in range(V)]
            near = [around(h, k) for h in hat]
            for i in range(V):
                r[i * H + n] = (
                    old[i]
                    - dot([(a[i * V + q], near[q][0]) for q in range(V)])
                    - dot([(c[i * V + q], near[q][1]) for q in range(V)])
                )
        near = [around(nn[e], k) for e in range(25)]
        minus_product(b, a, [v[0] for v in near])
        minus_product(c, c, [v[1] for v in near], keep=False, into=nn)
        near = [around(kk[e], k) for e in range(25)]
        minus_product(b, c, [v[1] for v in near])
        minus_product(a, a, [v[0] for v in near], keep=False)
        for e in range(25):
            c[e] = nn[e]
    invert()
    for e in range(25):
        a[e] = jnp.where(lower, c[e], a[e])
    left_apply(bi, a, kk)
    for n in range(H):
        old = [r[i * H + n] for i in range(V)]
        hat = [dot([(bi[i * V + q], old[q]) for q in range(V)]) for i in range(V)]
        other = [far(h) for h in hat]
        for i in range(V):
            r[i * H + n] = old[i] - dot([(a[i * V + q], other[q]) for q in range(V)])
    minus_product(b, a, [far(kk[e]) for e in range(25)])
    invert()
    for n in range(H):
        old = [r[i * H + n] for i in range(V)]
        for i in range(V):
            r[i * H + n] = dot([(bi[i * V + q], old[q]) for q in range(V)])


def close(b, c, r, fl, fh, first, edge, edge_ok):
    for i in range(V):
        h = jnp.where(edge_ok, edge(i), 0.0)
        for j in range(V):
            e = i * V + j
            c[e] = -(h * fh(e))
            b[e] = b[e] - h * fl(e)
        for n in range(H):
            r[i * H + n] = r[i * H + n] + h * first(i * H + n)


def x_solver_kernel(flag_ref, msg_ref, out_ref, a, b, c, r, kk, nn, bi):
    lanes, subs = lane(), sub()
    even = lanes < 64
    even = jnp.logical_xor(even, flag_ref[5] == 1)

    def pair(row):
        return [msg_ref[pl.ds(row + p * XR, 8, stride=2 * XR), :] for p in range(2)]

    def own(row):
        p, q = pair(row)
        return jnp.where(even, p, q)

    def following(row):
        p, q = pair(row)
        v = jnp.where(even, q, p)
        return jnp.where(even, v, pltpu.roll(v, 7, 0))

    def around(v, k):
        if k > 1:
            return pltpu.roll(v, k // 2, 0), pltpu.roll(v, 8 - k // 2, 0)
        v = swap(v)
        return jnp.where(even, pltpu.roll(v, 1, 0), v), jnp.where(even, v, pltpu.roll(v, 7, 0))

    def far(v):
        return pltpu.roll(v, 4, 0)

    begin = (subs == 0) & even
    end = (subs == 7) & jnp.logical_not(even)
    for e in range(25):
        a[e] = jnp.where(begin, 0.0, own(40 + e))
        b[e] = own(65 + e)
    for e in range(40):
        r[e] = own(e)
    close(
        b, c, r, lambda e: following(65 + e), lambda e: following(40 + e), following,
        lambda i: own(90 + i), jnp.logical_not(end),
    )
    reduce_lines(a, b, c, r, around, far, 4, kk, nn, bi, subs < 4)
    for e in range(40):
        u = r[e]
        v = swap(u)
        before = jnp.where(subs == 0, 0.0, pltpu.roll(v, 1, 0))
        out_ref[pl.ds(e, 8, stride=80), :] = jnp.where(even, before, v)
        out_ref[pl.ds(40 + e, 8, stride=80), :] = u


def y_solver_kernel(flag_ref, msg_ref, out_ref, a, b, c, r, kk, nn, bi, fh, fl):
    lanes, subs = lane(), sub()
    left = jnp.logical_xor(lanes < 64, flag_ref[6] == 1)

    def rhs(row):
        return msg_ref[pl.ds(row, 8, stride=YR), :]

    def following(v):
        return pltpu.roll(v, 7, 0)

    def pair(row):
        p = rhs(80 + row)
        q = swap(p)
        return jnp.where(left, p, q), jnp.where(left, q, p)

    def around(v, k):
        return pltpu.roll(v, k, 0), pltpu.roll(v, 8 - k, 0)

    begin = subs == 0
    for e in range(25):
        low, fh[e] = pair(e)
        a[e] = jnp.where(begin, 0.0, low)
        b[e], fl[e] = pair(25 + e)
    for e in range(40):
        r[e] = rhs(e)
    close(
        b, c, r, lambda e: following(fl[e]), lambda e: following(fh[e]),
        lambda e: following(rhs(40 + e)), lambda i: pair(50 + i)[0], subs != 7,
    )
    reduce_lines(a, b, c, r, around, lambda v: pltpu.roll(v, 4, 0), 3, kk, nn, bi, subs < 4)
    for e in range(40):
        u = r[e]
        out_ref[pl.ds(e, 8, stride=80), :] = jnp.where(begin, 0.0, pltpu.roll(u, 1, 0))
        out_ref[pl.ds(40 + e, 8, stride=80), :] = u


def middle_kernel(flag_ref, ret_ref, v_ref, fac_ref, h_ref, edge_ref):
    for y in range(B):
        prev, cur = [], []
        for i in range(V):
            um, u = [], []
            for ih in range(2):
                z = [ret_ref[y * 4 + 2 * zh + ih, i * H : (i + 1) * H, :] for zh in range(2)]
                p, q = join(*z)
                um.append(p)
                u.append(q)
            prev.append(jnp.concatenate(um, axis=0)[:N])
            cur.append(jnp.concatenate(u, axis=0)[:N])
        for t in range(B - 1):
            lo = apply(fac_ref, 3 + t, y, prev)
            hi = apply(fac_ref, 6 + t, y, cur)
            for i in range(V):
                h_ref[t, y, i] = v_ref[t, y, i] + lo[i] + hi[i]
        for i in range(V):
            h_ref[B - 1, y, i] = cur[i]
    edge_ref[...] = pack_edges(lambda x, y, i: h_ref[x, y, i], flag_ref[0])


def second_inner_kernel(
    omega_ref, h_ref, source_ref, r_ref, couple_ref, spec_ref, part_ref, table
):
    lanes = lane((N, 128))
    scaled_table(spec_ref, omega_ref, table)
    for x in range(B):
        for y in range(B):
            spec = spectral_terms(lambda i, k: h_ref[x, y, i, k : k + 1, :], table)
            h = [h_ref[x, y, i] for i in range(V)]
            for i in range(V):
                c = dot([(couple_ref[x, i, k, y : y + 1, :], h[k]) for k in range(V)])
                r = source_ref[x, y, i] - r_ref[x, y, i] + c
                part_ref[x, y, i] = r - h[i] + 0.5 * z_inner(h[i], lanes) - spec[i]


def second_kernel(flag_ref, part_ref, halo_ref, yf_ref, fac_ref, ymat_ref, v_ref, msg_ref):
    flag = flag_ref[0]
    lanes = lane((N, 128))
    halo = halo_ref[...]

    def right(x, t, i):
        return part_ref[x, t, i] + 0.5 * z_outer(halo, (x * B + t) * V + i, flag, lanes)

    for x in range(B):
        v0, v1, v2, last = condense(
            fac_ref, 4 + x,
            lambda t: [right(x, t, i) for i in range(V)],
            lambda t: [yf_ref[0, x, i, t : t + 1, :] for i in range(V)],
            lambda t: [yf_ref[1, x, i, t : t + 1, :] for i in range(V)],
        )
        for i in range(V):
            v_ref[x, 0, i] = v0[i]
            v_ref[x, 1, i] = v1[i]
            v_ref[x, 2, i] = v2[i]
            for at, v in ((0, last[i]), (40, v0[i])):
                for zh, m in enumerate(split(*halves(v))):
                    msg_ref[x * 2 + zh, at + i * H : at + (i + 1) * H, :] = m
    for d in range(8):
        msg_ref[d, 80:YR, :] = ymat_ref[d * MR : (d + 1) * MR, :]


def last_kernel(ret_ref, v_ref, fac_ref, w_ref):
    def put(x, y, i, v):
        w_ref[pl.ds((x * V + i) * N * B + y, N, stride=B), :] = v

    for x in range(B):
        prev, cur = [], []
        for i in range(V):
            for out, at in ((prev, 0), (cur, 40)):
                z = [ret_ref[x * 2 + zh, at + i * H : at + (i + 1) * H, :] for zh in range(2)]
                rows = join(*z)
                out.append(jnp.concatenate(rows, axis=0)[:N])
        for t in range(B - 1):
            lo = apply(fac_ref, 3 + t, 4 + x, prev)
            hi = apply(fac_ref, 6 + t, 4 + x, cur)
            for i in range(V):
                put(x, t, i, v_ref[x, t, i] + lo[i] + hi[i])
        for i in range(V):
            put(x, B - 1, i, cur[i])


smem = pl.BlockSpec(memory_space=pltpu.SMEM)
vmem = pl.BlockSpec(memory_space=pltpu.VMEM)


def sds(*shape):
    return jax.ShapeDtypeStruct(shape, f32)


def scratch(*shape):
    return pltpu.VMEM(shape, f32)


def call(kernel, ins, outs, scratches=(), **more):
    single = not isinstance(outs, (list, tuple))
    return pl.pallas_call(
        kernel,
        in_specs=list(ins),
        out_specs=vmem if single else [vmem] * len(outs),
        out_shape=outs,
        scratch_shapes=list(scratches),
        compiler_params=pltpu.CompilerParams(vmem_limit_bytes=40 * 2**20),
        **more,
    )


def cost(us):
    return pl.CostEstimate(flops=0, bytes_accessed=int(us * 3.6e6), transcendentals=0)


def body(state, source, x_faces, y_faces, couple, omega):
    n_y = lax.axis_size("gy")
    at_x = lax.axis_index("gx").astype(jnp.int32)
    at_y = lax.axis_index("gy").astype(jnp.int32)
    at_z = lax.axis_index("gz").astype(jnp.int32)
    flag = jnp.stack(
        [at_z, at_y & 1, at_y, jnp.full((), n_y, jnp.int32), at_x & 1, (at_x >> 1) & 1, at_y & 1]
    )
    spec = jnp.asarray(spectral_columns())
    pairs = [(i, i ^ 1) for i in range(n_y)]
    other_pairs = [(i, (i + 1) % n_y if i % 2 else (i - 1) % n_y) for i in range(n_y)]
    flip = [(0, 1), (1, 0)]
    field = sds(B, B, V, N, 128)
    mats = [scratch(25, 8, 128)] * 3 + [scratch(40, 8, 128)] + [scratch(25, 8, 128)] * 3

    rows = jnp.transpose(state, (0, 2, 3, 1, 4)).reshape(LINE, 128)
    near, far = call(
        edge_kernel, [smem, vmem], [sds(B, V, N, 128), sds(B, V, N, 128)]
    )(flag, rows)
    near = lax.ppermute(near, "gy", pairs)
    far = lax.ppermute(far, "gy", other_pairs)
    couple = jnp.transpose(couple, (0, 2, 3, 1, 4))
    x_faces = jnp.transpose(x_faces, (0, 1, 3, 2, 4))
    y_faces = jnp.transpose(y_faces, (0, 1, 3, 2, 4))
    fac, xmat, ymat, edge = call(
        matrix_kernel, [smem] + [vmem] * 4,
        [sds(225, 8, 128), sds(16 * MR, 128), sds(8 * MR, 128), sds(N, 128)],
        [scratch(B * 25 * 8, 128), scratch(B * V * 8, 128), scratch(B * V * 8, 128)],
        cost_estimate=cost(1),
    )(flag, state, couple, x_faces, y_faces)
    halo = lax.ppermute(edge, "gz", flip)
    part = call(
        inner_kernel, [smem] + [vmem] * 4, field, [scratch(N, N, 128)], cost_estimate=cost(1),
    )(omega, state, source, y_faces, spec)
    r1, v, msg = call(
        first_kernel, [smem] + [vmem] * 8,
        [field, sds(B - 1, B, V, N, 128), sds(16, XR, 128)],
    )(flag, part, near, far, halo, x_faces, y_faces, fac, xmat)
    got = lax.all_to_all(msg, "gx", 0, 0, tiled=True)
    ret = call(x_solver_kernel, [smem, vmem], sds(16 * 40, 128), mats)(
        flag, got.reshape(16 * XR, 128)
    )
    back = lax.all_to_all(ret.reshape(16, 40, 128), "gx", 0, 0, tiled=True)
    h, edge = call(middle_kernel, [smem, vmem, vmem, vmem], [field, sds(N, 128)])(
        flag, back, v, fac
    )
    halo = lax.ppermute(edge, "gz", flip)
    part = call(
        second_inner_kernel, [smem] + [vmem] * 5, field, [scratch(N, N, 128)],
        cost_estimate=cost(1),
    )(omega, h, source, r1, couple, spec)
    v, msg = call(
        second_kernel, [smem] + [vmem] * 5, [sds(B, B - 1, V, N, 128), sds(8, YR, 128)]
    )(flag, part, halo, y_faces, fac, ymat)
    got = lax.all_to_all(msg, "gy", 0, 0, tiled=True)
    ret = call(
        y_solver_kernel, [smem, vmem], sds(8 * 80, 128),
        mats + [scratch(25, 8, 128), scratch(25, 8, 128)],
    )(flag, got.reshape(8 * YR, 128))
    back = lax.all_to_all(ret.reshape(8, 80, 128), "gy", 0, 0, tiled=True)
    out = call(last_kernel, [vmem] * 3, sds(LINE, 128))(back, v, fac)
    return jnp.transpose(out.reshape(B, V, N, B, 128), (0, 3, 1, 2, 4))


def solution(mesh):
    return jax.shard_map(
        body,
        mesh=mesh,
        in_specs=(
            P("gx", "gy", None, None, "gz"),
            P("gx", "gy", None, None, "gz"),
            P(None, "gx", "gy", None, "gz"),
            P(None, "gx", "gy", None, "gz"),
            P("gx", "gy", None, None, "gz"),
            P(),
        ),
        out_specs=P("gx", "gy", None, None, "gz"),
        check_vma=False,
    )
```

```python
import functools
import math

import jax
import jax.numpy as jnp
from jax import lax
from jax.experimental import pallas as pl
from jax.experimental.pallas import tpu as pltpu
from jax.sharding import PartitionSpec as P


V = 5
N = 15
B = 4
H = 8
XR = 96
MR = 56
YR = 136
LINE = B * V * N * B
f32 = jnp.float32


def spectral_entry(gap):
    return 0.0 if gap == 0 else 0.5 * (-1) ** gap / math.sin(math.pi * gap / N)


def spectral_table(omega, table):
    subs = sub((N, 128))
    entries = {gap: omega * spectral_entry(gap) for gap in range(1 - N, N)}
    for k in range(N):
        column = jnp.zeros((N, 128), f32)
        for j in range(N):
            column = jnp.where(subs == j, entries[j - k], column)
        table[k] = column


def lane(shape=(8, 128)):
    return lax.broadcasted_iota(jnp.int32, shape, len(shape) - 1)


def sub(shape=(8, 128)):
    return lax.broadcasted_iota(jnp.int32, shape, len(shape) - 2)


def swap(v):
    return pltpu.roll(v, 64, 1)


def split(e0, e1):
    far, left = swap(e1), lane() < 64
    return jnp.where(left, e0, far), jnp.where(left, far, e0)


def join(z0, z1):
    left = lane() < 64
    return jnp.where(left, z0, z1), swap(jnp.where(left, z1, z0))


def choose(flag, p, q):
    return jnp.where(flag, q, p), jnp.where(flag, p, q)


def inverse(m):
    m = list(m)
    for p in range(V):
        piv = 1.0 / m[p * V + p]
        for j in range(V):
            if j != p:
                m[p * V + j] = m[p * V + j] * piv
        m[p * V + p] = piv
        for i in range(V):
            if i != p:
                f = m[i * V + p]
                for j in range(V):
                    if j != p:
                        m[i * V + j] = m[i * V + j] - f * m[p * V + j]
                m[i * V + p] = -f * piv
    return m


def dot(terms):
    total = None
    for a, b in terms:
        total = a * b if total is None else total + a * b
    return total


def matmul(a, b):
    return [
        dot([(a[i * V + k], b[k * V + j]) for k in range(V)]) for i in range(V) for j in range(V)
    ]


def edge_kernel(state_ref, near_ref, far_ref):
    even = lax.axis_index("gy") % 2 == 0
    for x in range(B):
        for i in range(V):
            at = (x * V + i) * N * B
            first = state_ref[pl.ds(at, N, stride=B), :]
            last = state_ref[pl.ds(at + B - 1, N, stride=B), :]
            near_ref[x, i], far_ref[x, i] = choose(even, first, last)


def pack_edges(load, flag):
    shift = jnp.where(flag == 0, 1, 0)
    lanes = lane((N, 128))
    acc = jnp.zeros((N, 128), f32)
    for c in range(B * B * V):
        x, y, i = c // (B * V), (c // V) % B, c % V
        acc = jnp.where(lanes == c, pltpu.roll(load(x, y, i), shift + c, 1), acc)
    return acc


def z_inner(v, lanes):
    low = jnp.where(lanes == 0, 0.0, pltpu.roll(v, 1, 1))
    high = jnp.where(lanes == 127, 0.0, pltpu.roll(v, 127, 1))
    return low + high


def z_outer(halo, c, flag, lanes):
    edge = jnp.where(flag == 0, 127, 0)
    shift = jnp.where(flag == 0, 127 - c, 128 - c)
    return jnp.where(lanes == edge, pltpu.roll(halo, shift, 1), 0.0)


def matrix_kernel(
    omega_ref, state_ref, couple_ref, xf_ref, yf_ref, fac_ref, xmat_ref, ymat_ref,
    edge_ref, table_ref, mel, lo, hi,
):
    spectral_table(omega_ref[0], table_ref)
    edge_ref[...] = pack_edges(lambda x, y, i: state_ref[x, y, i], lax.axis_index("gz"))
    for a in range(B):
        for i in range(V):
            for j in range(V):
                c = couple_ref[a, i, j]
                e = i * V + j
                mel[(a * 25 + e) * 8 : (a * 25 + e) * 8 + 4, :] = c
                mel[pl.ds(e * 8 + 4 + a, B, stride=25 * 8), :] = c
            lo[(a * V + i) * 8 : (a * V + i) * 8 + 4, :] = xf_ref[0, a, i]
            hi[(a * V + i) * 8 : (a * V + i) * 8 + 4, :] = xf_ref[1, a, i]
            lo[pl.ds(i * 8 + 4 + a, B, stride=V * 8), :] = yf_ref[0, a, i]
            hi[pl.ds(i * 8 + 4 + a, B, stride=V * 8), :] = yf_ref[1, a, i]

    def row(ref, r):
        return ref[r * 8 : r * 8 + 8, :]

    low = [[row(lo, t * V + i) for i in range(V)] for t in range(B)]
    high = [[row(hi, t * V + i) for i in range(V)] for t in range(B)]

    def mid(t):
        m = [row(mel, t * 25 + e) for e in range(25)]
        for i in range(V):
            m[i * V + i] = m[i * V + i] + (low[t][i] + high[t][i])
        return m

    def put(block, m):
        for e in range(25):
            fac_ref[block * 25 + e] = m[e]

    def get(block):
        return [fac_ref[block * 25 + e] for e in range(25)]

    def rows_by(d, m):
        return [d[i] * m[i * V + j] for i in range(V) for j in range(V)]

    def cols_by(m, d):
        return [m[i * V + j] * d[j] for i in range(V) for j in range(V)]

    g0 = inverse(mid(0))
    put(0, g0)
    m1 = mid(1)
    s = rows_by(low[1], cols_by(g0, high[0]))
    g1 = inverse([p - q for p, q in zip(m1, s)])
    put(1, g1)
    m2 = mid(2)
    s = rows_by(low[2], cols_by(g1, high[1]))
    g2 = inverse([p - q for p, q in zip(m2, s)])
    put(2, g2)
    e2 = cols_by(g2, high[2])
    put(8, e2)
    e1 = matmul(get(1), rows_by(high[1], e2))
    put(7, e1)
    e0 = matmul(get(0), rows_by(high[0], e1))
    put(6, e0)
    l0 = cols_by(get(0), low[0])
    l1 = matmul(get(1), rows_by(low[1], l0))
    l2 = matmul(get(2), rows_by(low[2], l1))
    put(5, l2)
    b1 = matmul(get(1), rows_by(high[1], l2))
    l1 = [p + q for p, q in zip(l1, b1)]
    put(4, l1)
    b0 = matmul(get(0), rows_by(high[0], l1))
    l0 = [p + q for p, q in zip(cols_by(get(0), low[0]), b0)]
    put(3, l0)

    lanes = lane()
    m3 = mid(3)
    last_low, last_high = get(5), get(8)
    first_low, first_high = get(3), get(6)

    blocks = [[], [], [], []]
    for i in range(V):
        for j in range(V):
            e = i * V + j
            blocks[0].append(-(low[3][i] * last_low[e]))
            blocks[1].append(m3[e] - low[3][i] * last_high[e])
            blocks[2].append(first_low[e])
            blocks[3].append(first_high[e])
    zero = jnp.zeros((8, 128), f32)
    edge = [high[3][i] for i in range(V)]
    odd = lax.axis_index("gx") % 2 == 1
    for r in range(55):
        if r < 50:
            e0, e1 = blocks[0 if r < 25 else 1][r % 25], blocks[3 if r < 25 else 2][r % 25]
        else:
            e0, e1 = edge[r - 50], zero
        for zh, v in enumerate(split(*choose(odd, e0, e1))):
            xmat_ref[pl.ds(zh * MR + r, 4, stride=2 * MR), :] = v[0:4]
        for zh, v in enumerate(split(e0, e1)):
            ymat_ref[pl.ds(zh * MR + r, 4, stride=2 * MR), :] = v[4:8]
    for d in range(8):
        xmat_ref[d * MR + 55 : (d + 1) * MR, :] = jnp.zeros((1, 128), f32)
        ymat_ref[d * MR + 55 : (d + 1) * MR, :] = jnp.zeros((1, 128), f32)


def halves(v):
    return v[0:H], jnp.concatenate([v[H:N], jnp.zeros((1, 128), f32)], axis=0)


def apply(fac_ref, block, line, vec):
    out = []
    for i in range(V):
        out.append(
            dot([(fac_ref[block * 25 + i * V + k, line : line + 1, :], vec[k]) for k in range(V)])
        )
    return out


def condense(fac_ref, line, right, low, high):
    y0 = apply(fac_ref, 0, line, right(0))
    y1 = apply(fac_ref, 1, line, [r + l * y for r, l, y in zip(right(1), low(1), y0)])
    v2 = apply(fac_ref, 2, line, [r + l * y for r, l, y in zip(right(2), low(2), y1)])
    c1 = apply(fac_ref, 1, line, [h * v for h, v in zip(high(1), v2)])
    v1 = [p + q for p, q in zip(y1, c1)]
    c0 = apply(fac_ref, 0, line, [h * v for h, v in zip(high(0), v1)])
    v0 = [p + q for p, q in zip(y0, c0)]
    last = [r + l * v for r, l, v in zip(right(3), low(3), v2)]
    return v0, v1, v2, last


def spectral_terms(load, table, lanes_shape=(N, 128)):
    acc = [None] * V
    for k in range(N):
        t = table[k]
        for i in range(V):
            p = t * load(i, k)
            acc[i] = p if acc[i] is None else acc[i] + p
    return acc


def inner_kernel(state_ref, source_ref, yf_ref, table, r_ref):
    lanes = lane((N, 128))
    for y in range(B):
        for x in range(B):
            spec = spectral_terms(lambda i, k: state_ref[x, y, i, k : k + 1, :], table)
            for i in range(V):
                s = state_ref[x, y, i]
                yl = yf_ref[0, x, i, y : y + 1, :]
                yh = yf_ref[1, x, i, y : y + 1, :]
                r = source_ref[x, y, i] - (yl + yh + 1.0) * s + 0.5 * z_inner(s, lanes)
                if y > 0:
                    r = r + yl * state_ref[x, y - 1, i]
                if y < B - 1:
                    r = r + yh * state_ref[x, y + 1, i]
                r_ref[x, y, i] = r - spec[i]


def first_kernel(
    part_ref, near_ref, far_ref, halo_ref, xf_ref, yf_ref, fac_ref, xmat_ref,
    r_ref, v_ref, msg_ref,
):
    flag = lax.axis_index("gz")
    lanes = lane((N, 128))
    halo = halo_ref[...]
    at = lax.axis_index("gy")
    even, begin, end = at % 2 == 0, at == 0, at == lax.axis_size("gy") - 1
    odd = lax.axis_index("gx") % 2 == 1
    for y in range(B):
        for x in range(B):
            for i in range(V):
                r = part_ref[x, y, i] + 0.5 * z_outer(halo, (x * B + y) * V + i, flag, lanes)
                if y == 0:
                    below = jnp.where(even, far_ref[x, i], near_ref[x, i])
                    r = r + yf_ref[0, x, i, y : y + 1, :] * jnp.where(begin, 0.0, below)
                if y == B - 1:
                    above = jnp.where(even, near_ref[x, i], far_ref[x, i])
                    r = r + yf_ref[1, x, i, y : y + 1, :] * jnp.where(end, 0.0, above)
                r_ref[x, y, i] = r
    for y in range(B):
        v0, v1, v2, last = condense(
            fac_ref, y,
            lambda t: [r_ref[t, y, i] for i in range(V)],
            lambda t: [xf_ref[0, t, i, y : y + 1, :] for i in range(V)],
            lambda t: [xf_ref[1, t, i, y : y + 1, :] for i in range(V)],
        )
        for i in range(V):
            v_ref[0, y, i] = v0[i]
            v_ref[1, y, i] = v1[i]
            v_ref[2, y, i] = v2[i]
            for ih, (e0, e1) in enumerate(zip(halves(last[i]), halves(v0[i]))):
                for zh, v in enumerate(split(*choose(odd, e0, e1))):
                    msg_ref[y * 4 + zh * 2 + ih, i * H : (i + 1) * H, :] = v
    for d in range(16):
        msg_ref[d, 40:XR, :] = xmat_ref[d // 2 * MR : (d // 2 + 1) * MR, :]


def product(a, m):
    out = []
    for i in range(V):
        row = [a[i * V + k] for k in range(V)]
        out += [dot([(row[k], m[k * V + j]) for k in range(V)]) for j in range(V)]
    return out


def reduce_lines(a, b, c, r, prepare, before, after, far, steps, kk, nn, bi, lower):
    def invert():
        inv = inverse([b[e] for e in range(25)])
        for e in range(25):
            bi[e] = inv[e]

    def put(dst, m, sign=1):
        for e in range(25):
            dst[e] = m[e] if sign > 0 else -m[e]

    def subtract(m):
        for e in range(25):
            b[e] = b[e] - m[e]

    for step in range(steps - 1):
        k = 2**step

        def low(m):
            return [before(v, k) for v in m]

        def high(m):
            return [after(v, k) for v in m]

        invert()
        m = [prepare(bi[e], k) for e in range(25)]
        put(kk, product(a, low(m)))
        put(nn, product(c, high(m)))
        for n in range(H):
            old = [r[i * H + n] for i in range(V)]
            m = [prepare(v, k) for v in old]
            m = low(m), high(m)
            for i in range(V):
                r[i * H + n] = (
                    old[i]
                    - dot([(kk[i * V + q], m[0][q]) for q in range(V)])
                    - dot([(nn[i * V + q], m[1][q]) for q in range(V)])
                )
        m = [prepare(c[e], k) for e in range(25)]
        subtract(product(kk, low(m)))
        put(c, product(nn, high(m)), -1)
        m = [prepare(a[e], k) for e in range(25)]
        subtract(product(nn, high(m)))
        put(a, product(kk, low(m)), -1)
    invert()
    for e in range(25):
        a[e] = jnp.where(lower, c[e], a[e])
    put(kk, product(a, [far(bi[e]) for e in range(25)]))
    for n in range(H):
        old = [r[i * H + n] for i in range(V)]
        other = [far(v) for v in old]
        for i in range(V):
            r[i * H + n] = old[i] - dot([(kk[i * V + q], other[q]) for q in range(V)])
    subtract(product(kk, [far(a[e]) for e in range(25)]))
    invert()
    for n in range(H):
        old = [r[i * H + n] for i in range(V)]
        for i in range(V):
            r[i * H + n] = dot([(bi[i * V + q], old[q]) for q in range(V)])


def close(b, c, fl, fh, edge):
    for i in range(V):
        for j in range(V):
            e = i * V + j
            c[e] = -(edge[i] * fh[e])
            b[e] = b[e] - edge[i] * fl[e]


def x_solver_kernel(msg_ref, out_ref, a, b, c, r, kk, nn, bi, fh, fl):
    lanes, subs = lane(), sub()
    even = lanes < 64
    even = jnp.logical_xor(even, lax.axis_index("gx") // 2 % 2 == 1)

    def pair(row):
        return [msg_ref[pl.ds(row + p * XR, 8, stride=2 * XR), :] for p in range(2)]

    def own(p, q):
        return jnp.where(even, p, q)

    def following(p, q):
        v = jnp.where(even, q, p)
        return jnp.where(even, v, pltpu.roll(v, 7, 0))

    def prepare(v, k):
        return swap(v) if k == 1 else v

    def before(v, k):
        if k > 1:
            return pltpu.roll(v, k // 2, 0)
        return jnp.where(even, pltpu.roll(v, 1, 0), v)

    def after(v, k):
        if k > 1:
            return pltpu.roll(v, 8 - k // 2, 0)
        return jnp.where(even, v, pltpu.roll(v, 7, 0))

    def far(v):
        return pltpu.roll(v, 4, 0)

    begin = (subs == 0) & even
    end = (subs == 7) & jnp.logical_not(even)
    for e in range(25):
        p, q = pair(40 + e)
        a[e], fh[e] = jnp.where(begin, 0.0, own(p, q)), following(p, q)
        p, q = pair(65 + e)
        b[e], fl[e] = own(p, q), following(p, q)
    edge = [jnp.where(end, 0.0, own(*pair(90 + i))) for i in range(V)]
    close(b, c, fl, fh, edge)
    for e in range(40):
        p, q = pair(e)
        r[e] = own(p, q) + edge[e // H] * following(p, q)
    reduce_lines(a, b, c, r, prepare, before, after, far, 4, kk, nn, bi, subs < 4)
    for e in range(40):
        u = r[e]
        v = swap(u)
        before = jnp.where(subs == 0, 0.0, pltpu.roll(v, 1, 0))
        out_ref[pl.ds(e, 8, stride=80), :] = jnp.where(even, before, v)
        out_ref[pl.ds(40 + e, 8, stride=80), :] = u


def y_solver_kernel(msg_ref, out_ref, a, b, c, r, kk, nn, bi, fh, fl):
    lanes, subs = lane(), sub()
    left = jnp.logical_xor(lanes < 64, lax.axis_index("gy") % 2 == 1)

    def rhs(row):
        return msg_ref[pl.ds(row, 8, stride=YR), :]

    def following(v):
        return pltpu.roll(v, 7, 0)

    def pair(row):
        p = rhs(row)
        q = swap(p)
        return jnp.where(left, p, q), jnp.where(left, q, p)

    begin = subs == 0
    for e in range(25):
        low, high = pair(80 + e)
        a[e], fh[e] = jnp.where(begin, 0.0, low), following(high)
        b[e], high = pair(105 + e)
        fl[e] = following(high)
    edge = [jnp.where(subs == 7, 0.0, pair(130 + i)[0]) for i in range(V)]
    close(b, c, fl, fh, edge)
    for e in range(40):
        r[e] = rhs(e) + edge[e // H] * following(rhs(40 + e))
    reduce_lines(
        a, b, c, r, lambda v, k: v, lambda v, k: pltpu.roll(v, k, 0),
        lambda v, k: pltpu.roll(v, 8 - k, 0), lambda v: pltpu.roll(v, 4, 0),
        3, kk, nn, bi, subs < 4,
    )
    for e in range(40):
        u = r[e]
        out_ref[pl.ds(e, 8, stride=80), :] = jnp.where(begin, 0.0, pltpu.roll(u, 1, 0))
        out_ref[pl.ds(40 + e, 8, stride=80), :] = u


def middle_kernel(ret_ref, v_ref, fac_ref, h_ref, edge_ref):
    for y in range(B):
        prev, cur = [], []
        for i in range(V):
            um, u = [], []
            for ih in range(2):
                z = [ret_ref[y * 4 + 2 * zh + ih, i * H : (i + 1) * H, :] for zh in range(2)]
                p, q = join(*z)
                um.append(p)
                u.append(q)
            prev.append(jnp.concatenate(um, axis=0)[:N])
            cur.append(jnp.concatenate(u, axis=0)[:N])
        for t in range(B - 1):
            lo = apply(fac_ref, 3 + t, y, prev)
            hi = apply(fac_ref, 6 + t, y, cur)
            for i in range(V):
                h_ref[t, y, i] = v_ref[t, y, i] + lo[i] + hi[i]
        for i in range(V):
            h_ref[B - 1, y, i] = cur[i]
    edge_ref[...] = pack_edges(lambda x, y, i: h_ref[x, y, i], lax.axis_index("gz"))


def second_inner_kernel(h_ref, source_ref, r_ref, couple_ref, table, part_ref):
    lanes = lane((N, 128))
    for x in range(B):
        for y in range(B):
            spec = spectral_terms(lambda i, k: h_ref[x, y, i, k : k + 1, :], table)
            h = [h_ref[x, y, i] for i in range(V)]
            for i in range(V):
                c = dot([(couple_ref[x, i, k, y : y + 1, :], h[k]) for k in range(V)])
                r = source_ref[x, y, i] - r_ref[x, y, i] + c
                part_ref[x, y, i] = r - h[i] + 0.5 * z_inner(h[i], lanes) - spec[i]


def second_kernel(part_ref, halo_ref, yf_ref, fac_ref, ymat_ref, v_ref, msg_ref):
    flag = lax.axis_index("gz")
    lanes = lane((N, 128))
    halo = halo_ref[...]

    def right(x, t, i):
        return part_ref[x, t, i] + 0.5 * z_outer(halo, (x * B + t) * V + i, flag, lanes)

    for x in range(B):
        v0, v1, v2, last = condense(
            fac_ref, 4 + x,
            lambda t: [right(x, t, i) for i in range(V)],
            lambda t: [yf_ref[0, x, i, t : t + 1, :] for i in range(V)],
            lambda t: [yf_ref[1, x, i, t : t + 1, :] for i in range(V)],
        )
        for i in range(V):
            v_ref[x, 0, i] = v0[i]
            v_ref[x, 1, i] = v1[i]
            v_ref[x, 2, i] = v2[i]
            for at, v in ((0, last[i]), (40, v0[i])):
                for zh, m in enumerate(split(*halves(v))):
                    msg_ref[x * 2 + zh, at + i * H : at + (i + 1) * H, :] = m
    for d in range(8):
        msg_ref[d, 80:YR, :] = ymat_ref[d * MR : (d + 1) * MR, :]


def last_kernel(ret_ref, v_ref, fac_ref, w_ref):
    def put(x, y, i, v):
        w_ref[pl.ds((x * V + i) * N * B + y, N, stride=B), :] = v

    for x in range(B):
        prev, cur = [], []
        for i in range(V):
            for out, at in ((prev, 0), (cur, 40)):
                z = [ret_ref[x * 2 + zh, at + i * H : at + (i + 1) * H, :] for zh in range(2)]
                rows = join(*z)
                out.append(jnp.concatenate(rows, axis=0)[:N])
        for t in range(B - 1):
            lo = apply(fac_ref, 3 + t, 4 + x, prev)
            hi = apply(fac_ref, 6 + t, 4 + x, cur)
            for i in range(V):
                put(x, t, i, v_ref[x, t, i] + lo[i] + hi[i])
        for i in range(V):
            put(x, B - 1, i, cur[i])


smem = pl.BlockSpec(memory_space=pltpu.SMEM)
vmem = pl.BlockSpec(memory_space=pltpu.VMEM)


def sds(*shape):
    return jax.ShapeDtypeStruct(shape, f32)


def scratch(*shape):
    return pltpu.VMEM(shape, f32)


def call(kernel, ins, outs, scratches=(), **more):
    single = not isinstance(outs, (list, tuple))
    return pl.pallas_call(
        kernel,
        in_specs=list(ins),
        out_specs=vmem if single else [vmem] * len(outs),
        out_shape=outs,
        scratch_shapes=list(scratches),
        compiler_params=pltpu.CompilerParams(vmem_limit_bytes=40 * 2**20),
        **more,
    )


def cost(us):
    return pl.CostEstimate(flops=0, bytes_accessed=int(us * 3.6e6), transcendentals=0)


def body(state, source, x_faces, y_faces, couple, omega):
    n_y = lax.axis_size("gy")
    pairs = [(i, i ^ 1) for i in range(n_y)]
    other_pairs = [(i, (i + 1) % n_y if i % 2 else (i - 1) % n_y) for i in range(n_y)]
    flip = [(0, 1), (1, 0)]
    field = sds(B, B, V, N, 128)
    mats = [scratch(25, 8, 128)] * 3 + [scratch(40, 8, 128)] + [scratch(25, 8, 128)] * 3

    couple = jnp.transpose(couple, (0, 2, 3, 1, 4))
    x_faces = jnp.transpose(x_faces, (0, 1, 3, 2, 4))
    y_faces = jnp.transpose(y_faces, (0, 1, 3, 2, 4))
    rows = jnp.transpose(state, (0, 2, 3, 1, 4)).reshape(LINE, 128)
    near, far = call(edge_kernel, [vmem], [sds(B, V, N, 128), sds(B, V, N, 128)])(rows)
    near = lax.ppermute(near, "gy", pairs)
    far = lax.ppermute(far, "gy", other_pairs)
    fac, xmat, ymat, edge, table = call(
        matrix_kernel, [smem] + [vmem] * 4,
        [
            sds(225, 8, 128), sds(8 * MR, 128), sds(8 * MR, 128), sds(N, 128),
            sds(N, N, 128),
        ],
        [scratch(B * 25 * 8, 128), scratch(B * V * 8, 128), scratch(B * V * 8, 128)],
        cost_estimate=cost(1),
    )(omega, state, couple, x_faces, y_faces)
    halo = lax.ppermute(edge, "gz", flip)
    part = call(
        inner_kernel, [vmem] * 4, field, cost_estimate=cost(1)
    )(state, source, y_faces, table)
    r1, v, msg = call(
        first_kernel, [vmem] * 8,
        [field, sds(B - 1, B, V, N, 128), sds(16, XR, 128)],
    )(part, near, far, halo, x_faces, y_faces, fac, xmat)
    got = lax.all_to_all(msg, "gx", 0, 0, tiled=True)
    mats += [scratch(25, 8, 128)] * 2
    ret = call(x_solver_kernel, [vmem], sds(16 * 40, 128), mats)(got.reshape(16 * XR, 128))
    back = lax.all_to_all(ret.reshape(16, 40, 128), "gx", 0, 0, tiled=True)
    h, edge = call(middle_kernel, [vmem] * 3, [field, sds(N, 128)])(back, v, fac)
    halo = lax.ppermute(edge, "gz", flip)
    part = call(
        second_inner_kernel, [vmem] * 5, field, cost_estimate=cost(1)
    )(h, source, r1, couple, table)
    v, msg = call(
        second_kernel, [vmem] * 5, [sds(B, B - 1, V, N, 128), sds(8, YR, 128)]
    )(part, halo, y_faces, fac, ymat)
    got = lax.all_to_all(msg, "gy", 0, 0, tiled=True)
    ret = call(
        y_solver_kernel, [vmem], sds(8 * 80, 128), mats
    )(got.reshape(8 * YR, 128))
    back = lax.all_to_all(ret.reshape(8, 80, 128), "gy", 0, 0, tiled=True)
    out = call(last_kernel, [vmem] * 3, sds(LINE, 128))(back, v, fac)
    return jnp.transpose(out.reshape(B, V, N, B, 128), (0, 3, 1, 2, 4))


def solution(mesh):
    return jax.shard_map(
        body,
        mesh=mesh,
        in_specs=(
            P("gx", "gy", None, None, "gz"),
            P("gx", "gy", None, None, "gz"),
            P(None, "gx", "gy", None, "gz"),
            P(None, "gx", "gy", None, "gz"),
            P("gx", "gy", None, None, "gz"),
            P(),
        ),
        out_specs=P("gx", "gy", None, None, "gz"),
        check_vma=False,
    )
```

```python
import functools
import math

import jax
import jax.numpy as jnp
from jax import lax
from jax.experimental import pallas as pl
from jax.experimental.pallas import tpu as pltpu
from jax.sharding import PartitionSpec as P


V = 5
N = 15
B = 4
H = 8
XR = 96
MR = 56
YR = 136
LINE = B * V * N * B
f32 = jnp.float32


def spectral_entry(gap):
    return 0.0 if gap == 0 else 0.5 * (-1) ** gap / math.sin(math.pi * gap / N)


def spectral_table(omega, table):
    subs = sub((N, 128))
    entries = {gap: omega * spectral_entry(gap) for gap in range(1 - N, N)}
    for k in range(N):
        column = jnp.zeros((N, 128), f32)
        for j in range(N):
            column = jnp.where(subs == j, entries[j - k], column)
        table[k] = column


def lane(shape=(8, 128)):
    return lax.broadcasted_iota(jnp.int32, shape, len(shape) - 1)


def sub(shape=(8, 128)):
    return lax.broadcasted_iota(jnp.int32, shape, len(shape) - 2)


def swap(v):
    return pltpu.roll(v, 64, 1)


def split(e0, e1):
    far, left = swap(e1), lane() < 64
    return jnp.where(left, e0, far), jnp.where(left, far, e0)


def join(z0, z1):
    left = lane() < 64
    return jnp.where(left, z0, z1), swap(jnp.where(left, z1, z0))


def choose(flag, p, q):
    return jnp.where(flag, q, p), jnp.where(flag, p, q)


def inverse(m):
    m = list(m)
    for p in range(V):
        piv = 1.0 / m[p * V + p]
        for j in range(V):
            if j != p:
                m[p * V + j] = m[p * V + j] * piv
        m[p * V + p] = piv
        for i in range(V):
            if i != p:
                f = m[i * V + p]
                for j in range(V):
                    if j != p:
                        m[i * V + j] = m[i * V + j] - f * m[p * V + j]
                m[i * V + p] = -f * piv
    return m


def dot(terms):
    total = None
    for a, b in terms:
        total = a * b if total is None else total + a * b
    return total


def matmul(a, b):
    return [
        dot([(a[i * V + k], b[k * V + j]) for k in range(V)]) for i in range(V) for j in range(V)
    ]


def edge_kernel(state_ref, near_ref, far_ref):
    even = lax.axis_index("gy") % 2 == 0

    def line(at):
        p = state_ref[pl.ds(at, H, stride=B), :]
        q = state_ref[pl.ds(at + (N - H) * B, H, stride=B), :]
        return jnp.concatenate([p, q[2 * H - N :]], axis=0)

    for x in range(B):
        for i in range(V):
            at = (x * V + i) * N * B
            first, last = line(at), line(at + B - 1)
            near_ref[x, i], far_ref[x, i] = choose(even, first, last)


def pack_edges(load, flag):
    shift = jnp.where(flag == 0, 1, 0)
    lanes = lane((N, 128))
    acc = jnp.zeros((N, 128), f32)
    for c in range(B * B * V):
        x, y, i = c // (B * V), (c // V) % B, c % V
        acc = jnp.where(lanes == c, pltpu.roll(load(x, y, i), shift + c, 1), acc)
    return acc


def z_inner(v, lanes):
    low = jnp.where(lanes == 0, 0.0, pltpu.roll(v, 1, 1))
    high = jnp.where(lanes == 127, 0.0, pltpu.roll(v, 127, 1))
    return low + high


def z_outer(halo, c, flag, lanes):
    edge = jnp.where(flag == 0, 127, 0)
    shift = jnp.where(flag == 0, 127 - c, 128 - c)
    return jnp.where(lanes == edge, pltpu.roll(halo, shift, 1), 0.0)


def matrix_kernel(
    omega_ref, state_ref, couple_ref, xf_ref, yf_ref, fac_ref, xmat_ref, ymat_ref,
    edge_ref, table_ref, mel, lo, hi,
):
    spectral_table(omega_ref[0], table_ref)
    edge_ref[...] = pack_edges(lambda x, y, i: state_ref[x, y, i], lax.axis_index("gz"))
    for a in range(B):
        for i in range(V):
            for j in range(V):
                c = couple_ref[a, i, j]
                e = i * V + j
                mel[(a * 25 + e) * 8 : (a * 25 + e) * 8 + 4, :] = c
                mel[pl.ds(e * 8 + 4 + a, B, stride=25 * 8), :] = c
            lo[(a * V + i) * 8 : (a * V + i) * 8 + 4, :] = xf_ref[0, a, i]
            hi[(a * V + i) * 8 : (a * V + i) * 8 + 4, :] = xf_ref[1, a, i]
            lo[pl.ds(i * 8 + 4 + a, B, stride=V * 8), :] = yf_ref[0, a, i]
            hi[pl.ds(i * 8 + 4 + a, B, stride=V * 8), :] = yf_ref[1, a, i]

    def row(ref, r):
        return ref[r * 8 : r * 8 + 8, :]

    low = [[row(lo, t * V + i) for i in range(V)] for t in range(B)]
    high = [[row(hi, t * V + i) for i in range(V)] for t in range(B)]

    def mid(t):
        m = [row(mel, t * 25 + e) for e in range(25)]
        for i in range(V):
            m[i * V + i] = m[i * V + i] + (low[t][i] + high[t][i])
        return m

    def put(block, m):
        for e in range(25):
            fac_ref[block * 25 + e] = m[e]

    def get(block):
        return [fac_ref[block * 25 + e] for e in range(25)]

    def rows_by(d, m):
        return [d[i] * m[i * V + j] for i in range(V) for j in range(V)]

    def cols_by(m, d):
        return [m[i * V + j] * d[j] for i in range(V) for j in range(V)]

    g0 = inverse(mid(0))
    put(0, g0)
    m1 = mid(1)
    s = rows_by(low[1], cols_by(g0, high[0]))
    g1 = inverse([p - q for p, q in zip(m1, s)])
    put(1, g1)
    m2 = mid(2)
    s = rows_by(low[2], cols_by(g1, high[1]))
    g2 = inverse([p - q for p, q in zip(m2, s)])
    put(2, g2)
    e2 = cols_by(g2, high[2])
    put(8, e2)
    e1 = matmul(get(1), rows_by(high[1], e2))
    put(7, e1)
    e0 = matmul(get(0), rows_by(high[0], e1))
    put(6, e0)
    l0 = cols_by(get(0), low[0])
    l1 = matmul(get(1), rows_by(low[1], l0))
    l2 = matmul(get(2), rows_by(low[2], l1))
    put(5, l2)
    b1 = matmul(get(1), rows_by(high[1], l2))
    l1 = [p + q for p, q in zip(l1, b1)]
    put(4, l1)
    b0 = matmul(get(0), rows_by(high[0], l1))
    l0 = [p + q for p, q in zip(cols_by(get(0), low[0]), b0)]
    put(3, l0)

    lanes = lane()
    m3 = mid(3)
    last_low, last_high = get(5), get(8)
    first_low, first_high = get(3), get(6)

    blocks = [[], [], [], []]
    for i in range(V):
        for j in range(V):
            e = i * V + j
            blocks[0].append(-(low[3][i] * last_low[e]))
            blocks[1].append(m3[e] - low[3][i] * last_high[e])
            blocks[2].append(first_low[e])
            blocks[3].append(first_high[e])
    zero = jnp.zeros((8, 128), f32)
    edge = [high[3][i] for i in range(V)]
    odd = lax.axis_index("gx") % 2 == 1
    for r in range(55):
        if r < 50:
            e0, e1 = blocks[0 if r < 25 else 1][r % 25], blocks[3 if r < 25 else 2][r % 25]
        else:
            e0, e1 = edge[r - 50], zero
        for zh, v in enumerate(split(*choose(odd, e0, e1))):
            xmat_ref[pl.ds(zh * MR + r, 4, stride=2 * MR), :] = v[0:4]
        for zh, v in enumerate(split(e0, e1)):
            ymat_ref[pl.ds(zh * MR + r, 4, stride=2 * MR), :] = v[4:8]
    for d in range(8):
        xmat_ref[d * MR + 55 : (d + 1) * MR, :] = jnp.zeros((1, 128), f32)
        ymat_ref[d * MR + 55 : (d + 1) * MR, :] = jnp.zeros((1, 128), f32)


def halves(v):
    return v[0:H], jnp.concatenate([v[H:N], jnp.zeros((1, 128), f32)], axis=0)


def apply(fac_ref, block, line, vec):
    out = []
    for i in range(V):
        out.append(
            dot([(fac_ref[block * 25 + i * V + k, line : line + 1, :], vec[k]) for k in range(V)])
        )
    return out


def condense(fac_ref, at, right, low, high):
    lines = range(B)

    def each(block, vec):
        return [apply(fac_ref, block, at + n, vec[n]) for n in lines]

    def plus(p, weights, q):
        return [[a + w * b for a, w, b in zip(p[n], weights(n), q[n])] for n in lines]

    y0 = each(0, [right(n, 0) for n in lines])
    y1 = each(1, plus([right(n, 1) for n in lines], lambda n: low(n, 1), y0))
    v2 = each(2, plus([right(n, 2) for n in lines], lambda n: low(n, 2), y1))
    c1 = each(1, [[h * v for h, v in zip(high(n, 1), v2[n])] for n in lines])
    v1 = [[p + q for p, q in zip(y1[n], c1[n])] for n in lines]
    c0 = each(0, [[h * v for h, v in zip(high(n, 0), v1[n])] for n in lines])
    v0 = [[p + q for p, q in zip(y0[n], c0[n])] for n in lines]
    last = plus([right(n, 3) for n in lines], lambda n: low(n, 3), v2)
    return v0, v1, v2, last


def spectral_terms(load, table, lanes_shape=(N, 128)):
    acc = [None] * V
    for k in range(N):
        t = table[k]
        for i in range(V):
            p = t * load(i, k)
            acc[i] = p if acc[i] is None else acc[i] + p
    return acc


def inner_kernel(state_ref, source_ref, yf_ref, table, r_ref):
    lanes = lane((N, 128))
    for y in range(B):
        for x in range(B):
            spec = spectral_terms(lambda i, k: state_ref[x, y, i, k : k + 1, :], table)
            for i in range(V):
                s = state_ref[x, y, i]
                yl = yf_ref[0, x, i, y : y + 1, :]
                yh = yf_ref[1, x, i, y : y + 1, :]
                r = source_ref[x, y, i] - (yl + yh + 1.0) * s + 0.5 * z_inner(s, lanes)
                if y > 0:
                    r = r + yl * state_ref[x, y - 1, i]
                if y < B - 1:
                    r = r + yh * state_ref[x, y + 1, i]
                r_ref[x, y, i] = r - spec[i]


def first_kernel(
    part_ref, near_ref, far_ref, halo_ref, xf_ref, yf_ref, fac_ref, xmat_ref,
    r_ref, v_ref, msg_ref,
):
    flag = lax.axis_index("gz")
    lanes = lane((N, 128))
    halo = halo_ref[...]
    at = lax.axis_index("gy")
    even, begin, end = at % 2 == 0, at == 0, at == lax.axis_size("gy") - 1
    odd = lax.axis_index("gx") % 2 == 1
    for y in range(B):
        for x in range(B):
            for i in range(V):
                r = part_ref[x, y, i] + 0.5 * z_outer(halo, (x * B + y) * V + i, flag, lanes)
                if y == 0:
                    below = jnp.where(even, far_ref[x, i], near_ref[x, i])
                    r = r + yf_ref[0, x, i, y : y + 1, :] * jnp.where(begin, 0.0, below)
                if y == B - 1:
                    above = jnp.where(even, near_ref[x, i], far_ref[x, i])
                    r = r + yf_ref[1, x, i, y : y + 1, :] * jnp.where(end, 0.0, above)
                r_ref[x, y, i] = r
    v0, v1, v2, last = condense(
        fac_ref, 0,
        lambda y, t: [r_ref[t, y, i] for i in range(V)],
        lambda y, t: [xf_ref[0, t, i, y : y + 1, :] for i in range(V)],
        lambda y, t: [xf_ref[1, t, i, y : y + 1, :] for i in range(V)],
    )
    for y in range(B):
        for i in range(V):
            v_ref[0, y, i] = v0[y][i]
            v_ref[1, y, i] = v1[y][i]
            v_ref[2, y, i] = v2[y][i]
            for ih, (e0, e1) in enumerate(zip(halves(last[y][i]), halves(v0[y][i]))):
                for zh, v in enumerate(split(*choose(odd, e0, e1))):
                    msg_ref[y * 4 + zh * 2 + ih, i * H : (i + 1) * H, :] = v
    for d in range(16):
        msg_ref[d, 40:XR, :] = xmat_ref[d // 2 * MR : (d // 2 + 1) * MR, :]


def product(a, m):
    out = []
    for i in range(V):
        row = [a[i * V + k] for k in range(V)]
        out += [dot([(row[k], m[k * V + j]) for k in range(V)]) for j in range(V)]
    return out


def reduce_lines(a, b, c, r, prepare, before, after, far, steps, kk, nn, bi, lower):
    def invert():
        inv = inverse([b[e] for e in range(25)])
        for e in range(25):
            bi[e] = inv[e]

    def put(dst, m, sign=1):
        for e in range(25):
            dst[e] = m[e] if sign > 0 else -m[e]

    def subtract(m):
        for e in range(25):
            b[e] = b[e] - m[e]

    invert()
    for step in range(steps - 1):
        k = 2**step

        def low(m):
            return [before(v, k) for v in m]

        def high(m):
            return [after(v, k) for v in m]

        m = [prepare(bi[e], k) for e in range(25)]
        put(kk, product(a, low(m)))
        put(nn, product(c, high(m)))
        mc = [prepare(c[e], k) for e in range(25)]
        subtract(product(kk, low(mc)))
        ma = [prepare(a[e], k) for e in range(25)]
        subtract(product(nn, high(ma)))
        invert()
        put(c, product(nn, high(mc)), -1)
        put(a, product(kk, low(ma)), -1)
        for n in range(H):
            old = [r[i * H + n] for i in range(V)]
            m = [prepare(v, k) for v in old]
            m = low(m), high(m)
            for i in range(V):
                r[i * H + n] = (
                    old[i]
                    - dot([(kk[i * V + q], m[0][q]) for q in range(V)])
                    - dot([(nn[i * V + q], m[1][q]) for q in range(V)])
                )
    for e in range(25):
        a[e] = jnp.where(lower, c[e], a[e])
    put(kk, product(a, [far(bi[e]) for e in range(25)]))
    subtract(product(kk, [far(a[e]) for e in range(25)]))
    invert()
    for n in range(H):
        old = [r[i * H + n] for i in range(V)]
        other = [far(v) for v in old]
        for i in range(V):
            r[i * H + n] = old[i] - dot([(kk[i * V + q], other[q]) for q in range(V)])
    for n in range(H):
        old = [r[i * H + n] for i in range(V)]
        for i in range(V):
            r[i * H + n] = dot([(bi[i * V + q], old[q]) for q in range(V)])


def places():
    return (sub() + 4 * lax.axis_index("gz")) % 8


def close(b, c, fl, fh, edge):
    for i in range(V):
        for j in range(V):
            e = i * V + j
            c[e] = -(edge[i] * fh[e])
            b[e] = b[e] - edge[i] * fl[e]


def x_solver_kernel(msg_ref, out_ref, a, b, c, r, kk, nn, bi, fh, fl):
    lanes, subs = lane(), places()
    even = lanes < 64
    even = jnp.logical_xor(even, lax.axis_index("gx") // 2 % 2 == 1)

    def pair(row):
        return [msg_ref[pl.ds(row + p * XR, 8, stride=2 * XR), :] for p in range(2)]

    def own(p, q):
        return jnp.where(even, p, q)

    def following(p, q):
        v = jnp.where(even, q, p)
        return jnp.where(even, v, pltpu.roll(v, 7, 0))

    def prepare(v, k):
        return swap(v) if k == 1 else v

    def before(v, k):
        if k > 1:
            return pltpu.roll(v, k // 2, 0)
        return jnp.where(even, pltpu.roll(v, 1, 0), v)

    def after(v, k):
        if k > 1:
            return pltpu.roll(v, 8 - k // 2, 0)
        return jnp.where(even, v, pltpu.roll(v, 7, 0))

    def far(v):
        return pltpu.roll(v, 4, 0)

    begin = (subs == 0) & even
    end = (subs == 7) & jnp.logical_not(even)
    for e in range(25):
        p, q = pair(40 + e)
        a[e], fh[e] = jnp.where(begin, 0.0, own(p, q)), following(p, q)
        p, q = pair(65 + e)
        b[e], fl[e] = own(p, q), following(p, q)
    edge = [jnp.where(end, 0.0, own(*pair(90 + i))) for i in range(V)]
    close(b, c, fl, fh, edge)
    for e in range(40):
        p, q = pair(e)
        r[e] = own(p, q) + edge[e // H] * following(p, q)
    reduce_lines(a, b, c, r, prepare, before, after, far, 4, kk, nn, bi, subs < 4)
    for e in range(40):
        u = r[e]
        v = swap(u)
        before = jnp.where(subs == 0, 0.0, pltpu.roll(v, 1, 0))
        out_ref[pl.ds(e, 8, stride=80), :] = jnp.where(even, before, v)
        out_ref[pl.ds(40 + e, 8, stride=80), :] = u


def y_solver_kernel(msg_ref, out_ref, a, b, c, r, kk, nn, bi, fh, fl):
    lanes, subs = lane(), places()
    left = jnp.logical_xor(lanes < 64, lax.axis_index("gy") % 2 == 1)

    def rhs(row):
        return msg_ref[pl.ds(row, 8, stride=YR), :]

    def following(v):
        return pltpu.roll(v, 7, 0)

    def pair(row):
        p = rhs(row)
        q = swap(p)
        return jnp.where(left, p, q), jnp.where(left, q, p)

    begin = subs == 0
    for e in range(25):
        low, high = pair(80 + e)
        a[e], fh[e] = jnp.where(begin, 0.0, low), following(high)
        b[e], high = pair(105 + e)
        fl[e] = following(high)
    edge = [jnp.where(subs == 7, 0.0, pair(130 + i)[0]) for i in range(V)]
    close(b, c, fl, fh, edge)
    for e in range(40):
        r[e] = rhs(e) + edge[e // H] * following(rhs(40 + e))
    reduce_lines(
        a, b, c, r, lambda v, k: v, lambda v, k: pltpu.roll(v, k, 0),
        lambda v, k: pltpu.roll(v, 8 - k, 0), lambda v: pltpu.roll(v, 4, 0),
        3, kk, nn, bi, subs < 4,
    )
    for e in range(40):
        u = r[e]
        out_ref[pl.ds(e, 8, stride=80), :] = jnp.where(begin, 0.0, pltpu.roll(u, 1, 0))
        out_ref[pl.ds(40 + e, 8, stride=80), :] = u


def middle_kernel(ret_ref, v_ref, fac_ref, h_ref, edge_ref):
    for y in range(B):
        prev, cur = [], []
        for i in range(V):
            um, u = [], []
            for ih in range(2):
                z = [ret_ref[y * 4 + 2 * zh + ih, i * H : (i + 1) * H, :] for zh in range(2)]
                p, q = join(*z)
                um.append(p)
                u.append(q)
            prev.append(jnp.concatenate(um, axis=0)[:N])
            cur.append(jnp.concatenate(u, axis=0)[:N])
        for t in range(B - 1):
            lo = apply(fac_ref, 3 + t, y, prev)
            hi = apply(fac_ref, 6 + t, y, cur)
            for i in range(V):
                h_ref[t, y, i] = v_ref[t, y, i] + lo[i] + hi[i]
        for i in range(V):
            h_ref[B - 1, y, i] = cur[i]
    edge_ref[...] = pack_edges(lambda x, y, i: h_ref[x, y, i], lax.axis_index("gz"))


def second_inner_kernel(h_ref, source_ref, r_ref, couple_ref, table, part_ref):
    lanes = lane((N, 128))
    for x in range(B):
        for y in range(B):
            spec = spectral_terms(lambda i, k: h_ref[x, y, i, k : k + 1, :], table)
            h = [h_ref[x, y, i] for i in range(V)]
            for i in range(V):
                c = dot([(couple_ref[x, i, k, y : y + 1, :], h[k]) for k in range(V)])
                r = source_ref[x, y, i] - r_ref[x, y, i] + c
                part_ref[x, y, i] = r - h[i] + 0.5 * z_inner(h[i], lanes) - spec[i]


def second_kernel(part_ref, halo_ref, yf_ref, fac_ref, ymat_ref, v_ref, msg_ref):
    flag = lax.axis_index("gz")
    lanes = lane((N, 128))
    halo = halo_ref[...]

    def right(x, t, i):
        return part_ref[x, t, i] + 0.5 * z_outer(halo, (x * B + t) * V + i, flag, lanes)

    v0, v1, v2, last = condense(
        fac_ref, 4,
        lambda x, t: [right(x, t, i) for i in range(V)],
        lambda x, t: [yf_ref[0, x, i, t : t + 1, :] for i in range(V)],
        lambda x, t: [yf_ref[1, x, i, t : t + 1, :] for i in range(V)],
    )
    for x in range(B):
        for i in range(V):
            v_ref[x, 0, i] = v0[x][i]
            v_ref[x, 1, i] = v1[x][i]
            v_ref[x, 2, i] = v2[x][i]
            for at, v in ((0, last[x][i]), (40, v0[x][i])):
                for zh, m in enumerate(split(*halves(v))):
                    msg_ref[x * 2 + zh, at + i * H : at + (i + 1) * H, :] = m
    for d in range(8):
        msg_ref[d, 80:YR, :] = ymat_ref[d * MR : (d + 1) * MR, :]


def last_kernel(ret_ref, v_ref, fac_ref, w_ref):
    def put(x, y, i, v):
        at = (x * V + i) * N * B + y
        w_ref[pl.ds(at, H, stride=B), :] = v[:H]
        w_ref[pl.ds(at + (N - H) * B, H, stride=B), :] = v[N - H :]

    for x in range(B):
        prev, cur = [], []
        for i in range(V):
            for out, at in ((prev, 0), (cur, 40)):
                z = [ret_ref[x * 2 + zh, at + i * H : at + (i + 1) * H, :] for zh in range(2)]
                rows = join(*z)
                out.append(jnp.concatenate(rows, axis=0)[:N])
        for t in range(B - 1):
            lo = apply(fac_ref, 3 + t, 4 + x, prev)
            hi = apply(fac_ref, 6 + t, 4 + x, cur)
            for i in range(V):
                put(x, t, i, v_ref[x, t, i] + lo[i] + hi[i])
        for i in range(V):
            put(x, B - 1, i, cur[i])


smem = pl.BlockSpec(memory_space=pltpu.SMEM)
vmem = pl.BlockSpec(memory_space=pltpu.VMEM)


def sds(*shape):
    return jax.ShapeDtypeStruct(shape, f32)


def scratch(*shape):
    return pltpu.VMEM(shape, f32)


def call(kernel, ins, outs, scratches=(), **more):
    single = not isinstance(outs, (list, tuple))
    return pl.pallas_call(
        kernel,
        in_specs=list(ins),
        out_specs=vmem if single else [vmem] * len(outs),
        out_shape=outs,
        scratch_shapes=list(scratches),
        compiler_params=pltpu.CompilerParams(vmem_limit_bytes=40 * 2**20),
        **more,
    )


def exchange(msg, axis):
    n = lax.axis_size(axis)
    groups = [[2 * i for i in range(n)], [2 * ((i + n // 2) % n) + 1 for i in range(n)]]
    return lax.all_to_all(msg, (axis, "gz"), 0, 0, tiled=True, axis_index_groups=groups)


def cost(us):
    return pl.CostEstimate(flops=0, bytes_accessed=int(us * 3.6e6), transcendentals=0)


def body(state, source, x_faces, y_faces, couple, omega):
    n_y = lax.axis_size("gy")
    pairs = [(i, i ^ 1) for i in range(n_y)]
    other_pairs = [(i, (i + 1) % n_y if i % 2 else (i - 1) % n_y) for i in range(n_y)]
    flip = [(0, 1), (1, 0)]
    field = sds(B, B, V, N, 128)
    mats = [scratch(25, 8, 128)] * 3 + [scratch(40, 8, 128)] + [scratch(25, 8, 128)] * 3

    couple = jnp.transpose(couple, (0, 2, 3, 1, 4))
    x_faces = jnp.transpose(x_faces, (0, 1, 3, 2, 4))
    y_faces = jnp.transpose(y_faces, (0, 1, 3, 2, 4))
    rows = jnp.transpose(state, (0, 2, 3, 1, 4)).reshape(LINE, 128)
    near, far = call(edge_kernel, [vmem], [sds(B, V, N, 128), sds(B, V, N, 128)])(rows)
    near = lax.ppermute(near, "gy", pairs)
    far = lax.ppermute(far, "gy", other_pairs)
    fac, xmat, ymat, edge, table = call(
        matrix_kernel, [smem] + [vmem] * 4,
        [
            sds(225, 8, 128), sds(16 * MR, 128), sds(16 * MR, 128), sds(N, 128),
            sds(N, N, 128),
        ],
        [scratch(2 * B * 25 * 8, 128)] + [scratch(2 * B * V * 8, 128)] * 2,
        cost_estimate=cost(1),
    )(omega, state, couple, x_faces, y_faces)
    halo = lax.ppermute(edge, "gz", flip)
    part = call(
        inner_kernel, [vmem] * 4, field, cost_estimate=cost(1)
    )(state, source, y_faces, table)
    r1, v, msg = call(
        first_kernel, [vmem] * 8,
        [field, sds(B - 1, B, V, N, 128), sds(16, XR, 128)],
    )(part, near, far, halo, x_faces, y_faces, fac, xmat)
    got = exchange(msg, "gx")
    mats += [scratch(25, 8, 128)] * 2
    ret = call(x_solver_kernel, [vmem], sds(16 * 40, 128), mats)(got.reshape(16 * XR, 128))
    back = exchange(ret.reshape(16, 40, 128), "gx")
    h, edge = call(middle_kernel, [vmem] * 3, [field, sds(N, 128)])(back, v, fac)
    halo = lax.ppermute(edge, "gz", flip)
    part = call(
        second_inner_kernel, [vmem] * 5, field, cost_estimate=cost(1)
    )(h, source, r1, couple, table)
    v, msg = call(
        second_kernel, [vmem] * 5, [sds(B, B - 1, V, N, 128), sds(8, YR, 128)]
    )(part, halo, y_faces, fac, ymat)
    got = exchange(msg, "gy")
    ret = call(
        y_solver_kernel, [vmem], sds(8 * 80, 128), mats
    )(got.reshape(8 * YR, 128))
    back = exchange(ret.reshape(8, 80, 128), "gy")
    out = call(last_kernel, [vmem] * 3, sds(LINE, 128))(back, v, fac)
    return jnp.transpose(out.reshape(B, V, N, B, 128), (0, 3, 1, 2, 4))


def solution(mesh):
    return jax.shard_map(
        body,
        mesh=mesh,
        in_specs=(
            P("gx", "gy", None, None, "gz"),
            P("gx", "gy", None, None, "gz"),
            P(None, "gx", "gy", None, "gz"),
            P(None, "gx", "gy", None, "gz"),
            P("gx", "gy", None, None, "gz"),
            P(),
        ),
        out_specs=P("gx", "gy", None, None, "gz"),
        check_vma=False,
    )
```

```python
import functools
import math

import jax
import jax.numpy as jnp
from jax import lax
from jax.experimental import pallas as pl
from jax.experimental.pallas import tpu as pltpu
from jax.sharding import PartitionSpec as P


V = 5
N = 15
B = 4
H = 8
XR = 96
MR = 56
YR = 128
YM = 48
LINE = B * V * N * B
f32 = jnp.float32


def spectral_entry(gap):
    return 0.0 if gap == 0 else 0.5 * (-1) ** gap / math.sin(math.pi * gap / N)


def spectral_table(omega, table):
    subs = sub((N, 128))
    entries = {gap: omega * spectral_entry(gap) for gap in range(1 - N, N)}
    for k in range(N):
        column = jnp.zeros((N, 128), f32)
        for j in range(N):
            column = jnp.where(subs == j, entries[j - k], column)
        table[k] = column


def lane(shape=(8, 128)):
    return lax.broadcasted_iota(jnp.int32, shape, len(shape) - 1)


def sub(shape=(8, 128)):
    return lax.broadcasted_iota(jnp.int32, shape, len(shape) - 2)


def swap(v):
    return pltpu.roll(v, 64, 1)


def split(e0, e1):
    far, left = swap(e1), lane() < 64
    return jnp.where(left, e0, far), jnp.where(left, far, e0)


def join(z0, z1):
    left = lane() < 64
    return jnp.where(left, z0, z1), swap(jnp.where(left, z1, z0))


def choose(flag, p, q):
    return jnp.where(flag, q, p), jnp.where(flag, p, q)


def inverse(m):
    m = list(m)
    for p in range(V):
        piv = 1.0 / m[p * V + p]
        for j in range(V):
            if j != p:
                m[p * V + j] = m[p * V + j] * piv
        m[p * V + p] = piv
        for i in range(V):
            if i != p:
                f = m[i * V + p]
                for j in range(V):
                    if j != p:
                        m[i * V + j] = m[i * V + j] - f * m[p * V + j]
                m[i * V + p] = -f * piv
    return m


def dot(terms):
    total = None
    for a, b in terms:
        total = a * b if total is None else total + a * b
    return total


def matmul(a, b):
    return [
        dot([(a[i * V + k], b[k * V + j]) for k in range(V)]) for i in range(V) for j in range(V)
    ]


def edge_kernel(state_ref, near_ref, far_ref):
    even = lax.axis_index("gy") % 2 == 0
    for x in range(B):
        for i in range(V):
            at = (x * V + i) * N * B
            first = state_ref[pl.ds(at, N, stride=B), :]
            last = state_ref[pl.ds(at + B - 1, N, stride=B), :]
            near_ref[x, i], far_ref[x, i] = choose(even, first, last)


def pack_edges(load, flag):
    shift = jnp.where(flag == 0, 1, 0)
    lanes = lane((N, 128))
    acc = jnp.zeros((N, 128), f32)
    for c in range(B * B * V):
        x, y, i = c // (B * V), (c // V) % B, c % V
        acc = jnp.where(lanes == c, pltpu.roll(load(x, y, i), shift + c, 1), acc)
    return acc


def z_inner(v, lanes):
    low = jnp.where(lanes == 0, 0.0, pltpu.roll(v, 1, 1))
    high = jnp.where(lanes == 127, 0.0, pltpu.roll(v, 127, 1))
    return low + high


def z_outer(halo, c, flag, lanes):
    edge = jnp.where(flag == 0, 127, 0)
    shift = jnp.where(flag == 0, 127 - c, 128 - c)
    return jnp.where(lanes == edge, pltpu.roll(halo, shift, 1), 0.0)


def matrix_kernel(
    omega_ref, state_ref, couple_ref, xf_ref, yf_ref, fac_ref, xmat_ref, ymat_ref, tail_ref,
    edge_ref, table_ref, mel, lo, hi,
):
    spectral_table(omega_ref[0], table_ref)
    edge_ref[...] = pack_edges(lambda x, y, i: state_ref[x, y, i], lax.axis_index("gz"))
    for a in range(B):
        for i in range(V):
            for j in range(V):
                c = couple_ref[a, i, j]
                e = i * V + j
                mel[(a * 25 + e) * 8 : (a * 25 + e) * 8 + 4, :] = c
                mel[pl.ds(e * 8 + 4 + a, B, stride=25 * 8), :] = c
            lo[(a * V + i) * 8 : (a * V + i) * 8 + 4, :] = xf_ref[0, a, i]
            hi[(a * V + i) * 8 : (a * V + i) * 8 + 4, :] = xf_ref[1, a, i]
            lo[pl.ds(i * 8 + 4 + a, B, stride=V * 8), :] = yf_ref[0, a, i]
            hi[pl.ds(i * 8 + 4 + a, B, stride=V * 8), :] = yf_ref[1, a, i]

    def row(ref, r):
        return ref[r * 8 : r * 8 + 8, :]

    low = [[row(lo, t * V + i) for i in range(V)] for t in range(B)]
    high = [[row(hi, t * V + i) for i in range(V)] for t in range(B)]

    def mid(t):
        m = [row(mel, t * 25 + e) for e in range(25)]
        for i in range(V):
            m[i * V + i] = m[i * V + i] + (low[t][i] + high[t][i])
        return m

    def put(block, m):
        for e in range(25):
            fac_ref[block * 25 + e] = m[e]

    def get(block):
        return [fac_ref[block * 25 + e] for e in range(25)]

    def rows_by(d, m):
        return [d[i] * m[i * V + j] for i in range(V) for j in range(V)]

    def cols_by(m, d):
        return [m[i * V + j] * d[j] for i in range(V) for j in range(V)]

    g0 = inverse(mid(0))
    put(0, g0)
    m1 = mid(1)
    s = rows_by(low[1], cols_by(g0, high[0]))
    g1 = inverse([p - q for p, q in zip(m1, s)])
    put(1, g1)
    m2 = mid(2)
    s = rows_by(low[2], cols_by(g1, high[1]))
    g2 = inverse([p - q for p, q in zip(m2, s)])
    put(2, g2)
    e2 = cols_by(g2, high[2])
    put(8, e2)
    e1 = matmul(get(1), rows_by(high[1], e2))
    put(7, e1)
    e0 = matmul(get(0), rows_by(high[0], e1))
    put(6, e0)
    l0 = cols_by(get(0), low[0])
    l1 = matmul(get(1), rows_by(low[1], l0))
    l2 = matmul(get(2), rows_by(low[2], l1))
    put(5, l2)
    b1 = matmul(get(1), rows_by(high[1], l2))
    l1 = [p + q for p, q in zip(l1, b1)]
    put(4, l1)
    b0 = matmul(get(0), rows_by(high[0], l1))
    l0 = [p + q for p, q in zip(cols_by(get(0), low[0]), b0)]
    put(3, l0)

    lanes = lane()
    m3 = mid(3)
    last_low, last_high = get(5), get(8)
    first_low, first_high = get(3), get(6)

    blocks = [[], [], [], []]
    for i in range(V):
        for j in range(V):
            e = i * V + j
            blocks[0].append(-(low[3][i] * last_low[e]))
            blocks[1].append(m3[e] - low[3][i] * last_high[e])
            blocks[2].append(first_low[e])
            blocks[3].append(first_high[e])
    zero = jnp.zeros((8, 128), f32)
    edge = [high[3][i] for i in range(V)]
    odd = lax.axis_index("gx") % 2 == 1
    for r in range(55):
        if r < 50:
            e0, e1 = blocks[0 if r < 25 else 1][r % 25], blocks[3 if r < 25 else 2][r % 25]
        else:
            e0, e1 = edge[r - 50], zero
        for zh, v in enumerate(split(*choose(odd, e0, e1))):
            xmat_ref[pl.ds(zh * MR + r, 4, stride=2 * MR), :] = v[0:4]
        if r % 25 < 24 and r < 50:
            for zh, v in enumerate(split(e0, e1)):
                at = zh * YM + r - r // 25
                ymat_ref[pl.ds(at, 4, stride=2 * YM), :] = v[4:8]
    for d in range(8):
        xmat_ref[d * MR + 55 : (d + 1) * MR, :] = jnp.zeros((1, 128), f32)
    for k, e in enumerate(edge + [blocks[0][24], blocks[3][24], blocks[1][24], blocks[2][24]]):
        tail_ref[k] = e


def halves(v, tail=None):
    tail = jnp.zeros((1, 128), f32) if tail is None else tail
    return v[0:H], jnp.concatenate([v[H:N], tail], axis=0)


def apply(fac_ref, block, line, vec):
    out = []
    for i in range(V):
        out.append(
            dot([(fac_ref[block * 25 + i * V + k, line : line + 1, :], vec[k]) for k in range(V)])
        )
    return out


def condense(fac_ref, line, right, low, high):
    y0 = apply(fac_ref, 0, line, right(0))
    y1 = apply(fac_ref, 1, line, [r + l * y for r, l, y in zip(right(1), low(1), y0)])
    v2 = apply(fac_ref, 2, line, [r + l * y for r, l, y in zip(right(2), low(2), y1)])
    c1 = apply(fac_ref, 1, line, [h * v for h, v in zip(high(1), v2)])
    v1 = [p + q for p, q in zip(y1, c1)]
    c0 = apply(fac_ref, 0, line, [h * v for h, v in zip(high(0), v1)])
    v0 = [p + q for p, q in zip(y0, c0)]
    last = [r + l * v for r, l, v in zip(right(3), low(3), v2)]
    return v0, v1, v2, last


def spectral_terms(load, table, lanes_shape=(N, 128)):
    acc = [None] * V
    for k in range(N):
        t = table[k]
        for i in range(V):
            p = t * load(i, k)
            acc[i] = p if acc[i] is None else acc[i] + p
    return acc


def inner_kernel(state_ref, source_ref, yf_ref, table, r_ref):
    lanes = lane((N, 128))
    for y in range(B):
        for x in range(B):
            spec = spectral_terms(lambda i, k: state_ref[x, y, i, k : k + 1, :], table)
            for i in range(V):
                s = state_ref[x, y, i]
                yl = yf_ref[0, x, i, y : y + 1, :]
                yh = yf_ref[1, x, i, y : y + 1, :]
                r = source_ref[x, y, i] - (yl + yh + 1.0) * s + 0.5 * z_inner(s, lanes)
                if y > 0:
                    r = r + yl * state_ref[x, y - 1, i]
                if y < B - 1:
                    r = r + yh * state_ref[x, y + 1, i]
                r_ref[x, y, i] = r - spec[i]


def first_kernel(
    part_ref, near_ref, far_ref, halo_ref, xf_ref, yf_ref, fac_ref, xmat_ref,
    r_ref, v_ref, msg_ref,
):
    flag = lax.axis_index("gz")
    lanes = lane((N, 128))
    halo = halo_ref[...]
    at = lax.axis_index("gy")
    even, begin, end = at % 2 == 0, at == 0, at == lax.axis_size("gy") - 1
    odd = lax.axis_index("gx") % 2 == 1
    for y in range(B):
        for x in range(B):
            for i in range(V):
                r = part_ref[x, y, i] + 0.5 * z_outer(halo, (x * B + y) * V + i, flag, lanes)
                if y == 0:
                    below = jnp.where(even, far_ref[x, i], near_ref[x, i])
                    r = r + yf_ref[0, x, i, y : y + 1, :] * jnp.where(begin, 0.0, below)
                if y == B - 1:
                    above = jnp.where(even, near_ref[x, i], far_ref[x, i])
                    r = r + yf_ref[1, x, i, y : y + 1, :] * jnp.where(end, 0.0, above)
                r_ref[x, y, i] = r
    for y in range(B):
        v0, v1, v2, last = condense(
            fac_ref, y,
            lambda t: [r_ref[t, y, i] for i in range(V)],
            lambda t: [xf_ref[0, t, i, y : y + 1, :] for i in range(V)],
            lambda t: [xf_ref[1, t, i, y : y + 1, :] for i in range(V)],
        )
        for i in range(V):
            v_ref[0, y, i] = v0[i]
            v_ref[1, y, i] = v1[i]
            v_ref[2, y, i] = v2[i]
            for ih, (e0, e1) in enumerate(zip(halves(last[i]), halves(v0[i]))):
                for zh, v in enumerate(split(*choose(odd, e0, e1))):
                    msg_ref[y * 4 + zh * 2 + ih, i * H : (i + 1) * H, :] = v
    for d in range(16):
        msg_ref[d, 40:XR, :] = xmat_ref[d // 2 * MR : (d // 2 + 1) * MR, :]


def product(a, m):
    out = []
    for i in range(V):
        row = [a[i * V + k] for k in range(V)]
        out += [dot([(row[k], m[k * V + j]) for k in range(V)]) for j in range(V)]
    return out


def reduce_lines(a, b, c, r, prepare, before, after, far, steps, kk, nn, bi, lower):
    def invert():
        inv = inverse([b[e] for e in range(25)])
        for e in range(25):
            bi[e] = inv[e]

    def put(dst, m, sign=1):
        for e in range(25):
            dst[e] = m[e] if sign > 0 else -m[e]

    def subtract(m):
        for e in range(25):
            b[e] = b[e] - m[e]

    for step in range(steps - 1):
        k = 2**step

        def low(m):
            return [before(v, k) for v in m]

        def high(m):
            return [after(v, k) for v in m]

        invert()
        m = [prepare(bi[e], k) for e in range(25)]
        put(kk, product(a, low(m)))
        put(nn, product(c, high(m)))
        for n in range(H):
            old = [r[i * H + n] for i in range(V)]
            m = [prepare(v, k) for v in old]
            m = low(m), high(m)
            for i in range(V):
                r[i * H + n] = (
                    old[i]
                    - dot([(kk[i * V + q], m[0][q]) for q in range(V)])
                    - dot([(nn[i * V + q], m[1][q]) for q in range(V)])
                )
        m = [prepare(c[e], k) for e in range(25)]
        subtract(product(kk, low(m)))
        put(c, product(nn, high(m)), -1)
        m = [prepare(a[e], k) for e in range(25)]
        subtract(product(nn, high(m)))
        put(a, product(kk, low(m)), -1)
    invert()
    for e in range(25):
        a[e] = jnp.where(lower, c[e], a[e])
    put(kk, product(a, [far(bi[e]) for e in range(25)]))
    for n in range(H):
        old = [r[i * H + n] for i in range(V)]
        other = [far(v) for v in old]
        for i in range(V):
            r[i * H + n] = old[i] - dot([(kk[i * V + q], other[q]) for q in range(V)])
    subtract(product(kk, [far(a[e]) for e in range(25)]))
    invert()
    for n in range(H):
        old = [r[i * H + n] for i in range(V)]
        for i in range(V):
            r[i * H + n] = dot([(bi[i * V + q], old[q]) for q in range(V)])


def places():
    return (sub() + 4 * lax.axis_index("gz")) % 8


def close(b, c, fl, fh, edge):
    for i in range(V):
        for j in range(V):
            e = i * V + j
            c[e] = -(edge[i] * fh[e])
            b[e] = b[e] - edge[i] * fl[e]


def x_solver_kernel(msg_ref, out_ref, a, b, c, r, kk, nn, bi, fh, fl):
    lanes, subs = lane(), places()
    even = lanes < 64
    even = jnp.logical_xor(even, lax.axis_index("gx") // 2 % 2 == 1)

    def pair(row):
        return [msg_ref[pl.ds(row + p * XR, 8, stride=2 * XR), :] for p in range(2)]

    def own(p, q):
        return jnp.where(even, p, q)

    def following(p, q):
        v = jnp.where(even, q, p)
        return jnp.where(even, v, pltpu.roll(v, 7, 0))

    def prepare(v, k):
        return swap(v) if k == 1 else v

    def before(v, k):
        if k > 1:
            return pltpu.roll(v, k // 2, 0)
        return jnp.where(even, pltpu.roll(v, 1, 0), v)

    def after(v, k):
        if k > 1:
            return pltpu.roll(v, 8 - k // 2, 0)
        return jnp.where(even, v, pltpu.roll(v, 7, 0))

    def far(v):
        return pltpu.roll(v, 4, 0)

    begin = (subs == 0) & even
    end = (subs == 7) & jnp.logical_not(even)
    for e in range(25):
        p, q = pair(40 + e)
        a[e], fh[e] = jnp.where(begin, 0.0, own(p, q)), following(p, q)
        p, q = pair(65 + e)
        b[e], fl[e] = own(p, q), following(p, q)
    edge = [jnp.where(end, 0.0, own(*pair(90 + i))) for i in range(V)]
    close(b, c, fl, fh, edge)
    for e in range(40):
        p, q = pair(e)
        r[e] = own(p, q) + edge[e // H] * following(p, q)
    reduce_lines(a, b, c, r, prepare, before, after, far, 4, kk, nn, bi, subs < 4)
    for e in range(40):
        u = r[e]
        v = swap(u)
        before = jnp.where(subs == 0, 0.0, pltpu.roll(v, 1, 0))
        out_ref[pl.ds(e, 8, stride=80), :] = jnp.where(even, before, v)
        out_ref[pl.ds(40 + e, 8, stride=80), :] = u


def y_solver_kernel(msg_ref, out_ref, a, b, c, r, kk, nn, bi, fh, fl):
    lanes, subs = lane(), places()
    left = jnp.logical_xor(lanes < 64, lax.axis_index("gy") % 2 == 1)

    def rhs(row):
        return msg_ref[pl.ds(row, 8, stride=YR), :]

    def following(v):
        return pltpu.roll(v, 7, 0)

    def pair(row):
        p = rhs(row)
        q = swap(p)
        return jnp.where(left, p, q), jnp.where(left, q, p)

    begin = subs == 0
    for e in range(24):
        low, high = pair(80 + e)
        a[e], fh[e] = jnp.where(begin, 0.0, low), following(high)
        b[e], high = pair(104 + e)
        fl[e] = following(high)

    def tail(row):
        return pair(row * H + H - 1)[1]

    a[24], fh[24] = jnp.where(begin, 0.0, tail(5)), following(tail(6))
    b[24], fl[24] = tail(7), following(tail(8))
    edge = [jnp.where(subs == 7, 0.0, tail(i)) for i in range(V)]
    close(b, c, fl, fh, edge)
    for e in range(40):
        r[e] = rhs(e) + edge[e // H] * following(rhs(40 + e))
    reduce_lines(
        a, b, c, r, lambda v, k: v, lambda v, k: pltpu.roll(v, k, 0),
        lambda v, k: pltpu.roll(v, 8 - k, 0), lambda v: pltpu.roll(v, 4, 0),
        3, kk, nn, bi, subs < 4,
    )
    for e in range(40):
        u = r[e]
        out_ref[pl.ds(e, 8, stride=80), :] = jnp.where(begin, 0.0, pltpu.roll(u, 1, 0))
        out_ref[pl.ds(40 + e, 8, stride=80), :] = u


def middle_kernel(ret_ref, v_ref, fac_ref, h_ref, edge_ref):
    for y in range(B):
        prev, cur = [], []
        for i in range(V):
            um, u = [], []
            for ih in range(2):
                z = [ret_ref[y * 4 + 2 * zh + ih, i * H : (i + 1) * H, :] for zh in range(2)]
                p, q = join(*z)
                um.append(p)
                u.append(q)
            prev.append(jnp.concatenate(um, axis=0)[:N])
            cur.append(jnp.concatenate(u, axis=0)[:N])
        for t in range(B - 1):
            lo = apply(fac_ref, 3 + t, y, prev)
            hi = apply(fac_ref, 6 + t, y, cur)
            for i in range(V):
                h_ref[t, y, i] = v_ref[t, y, i] + lo[i] + hi[i]
        for i in range(V):
            h_ref[B - 1, y, i] = cur[i]
    edge_ref[...] = pack_edges(lambda x, y, i: h_ref[x, y, i], lax.axis_index("gz"))


def second_inner_kernel(h_ref, source_ref, r_ref, couple_ref, table, part_ref):
    lanes = lane((N, 128))
    for x in range(B):
        for y in range(B):
            spec = spectral_terms(lambda i, k: h_ref[x, y, i, k : k + 1, :], table)
            h = [h_ref[x, y, i] for i in range(V)]
            for i in range(V):
                c = dot([(couple_ref[x, i, k, y : y + 1, :], h[k]) for k in range(V)])
                r = source_ref[x, y, i] - r_ref[x, y, i] + c
                part_ref[x, y, i] = r - h[i] + 0.5 * z_inner(h[i], lanes) - spec[i]


def second_kernel(part_ref, halo_ref, yf_ref, fac_ref, ymat_ref, tail_ref, v_ref, msg_ref):
    flag = lax.axis_index("gz")
    lanes = lane((N, 128))
    halo = halo_ref[...]

    def right(x, t, i):
        return part_ref[x, t, i] + 0.5 * z_outer(halo, (x * B + t) * V + i, flag, lanes)

    for x in range(B):
        v0, v1, v2, last = condense(
            fac_ref, 4 + x,
            lambda t: [right(x, t, i) for i in range(V)],
            lambda t: [yf_ref[0, x, i, t : t + 1, :] for i in range(V)],
            lambda t: [yf_ref[1, x, i, t : t + 1, :] for i in range(V)],
        )
        for i in range(V):
            v_ref[x, 0, i] = v0[i]
            v_ref[x, 1, i] = v1[i]
            v_ref[x, 2, i] = v2[i]
            for at, v, k in ((0, last[i], i), (40, v0[i], 5 + i)):
                tail = tail_ref[k, 4 + x : 5 + x, :] if k < 9 else None
                for zh, m in enumerate(split(*halves(v, tail))):
                    msg_ref[x * 2 + zh, at + i * H : at + (i + 1) * H, :] = m
    for d in range(8):
        msg_ref[d, 80:YR, :] = ymat_ref[d * YM : (d + 1) * YM, :]


def last_kernel(ret_ref, v_ref, fac_ref, w_ref):
    def put(x, y, i, v):
        w_ref[pl.ds((x * V + i) * N * B + y, N, stride=B), :] = v

    for x in range(B):
        prev, cur = [], []
        for i in range(V):
            for out, at in ((prev, 0), (cur, 40)):
                z = [ret_ref[x * 2 + zh, at + i * H : at + (i + 1) * H, :] for zh in range(2)]
                rows = join(*z)
                out.append(jnp.concatenate(rows, axis=0)[:N])
        for t in range(B - 1):
            lo = apply(fac_ref, 3 + t, 4 + x, prev)
            hi = apply(fac_ref, 6 + t, 4 + x, cur)
            for i in range(V):
                put(x, t, i, v_ref[x, t, i] + lo[i] + hi[i])
        for i in range(V):
            put(x, B - 1, i, cur[i])


smem = pl.BlockSpec(memory_space=pltpu.SMEM)
vmem = pl.BlockSpec(memory_space=pltpu.VMEM)


def sds(*shape):
    return jax.ShapeDtypeStruct(shape, f32)


def scratch(*shape):
    return pltpu.VMEM(shape, f32)


def call(kernel, ins, outs, scratches=(), **more):
    single = not isinstance(outs, (list, tuple))
    return pl.pallas_call(
        kernel,
        in_specs=list(ins),
        out_specs=vmem if single else [vmem] * len(outs),
        out_shape=outs,
        scratch_shapes=list(scratches),
        compiler_params=pltpu.CompilerParams(vmem_limit_bytes=40 * 2**20),
        **more,
    )


def exchange(msg, axis):
    n = lax.axis_size(axis)
    groups = [[2 * i for i in range(n)], [2 * ((i + n // 2) % n) + 1 for i in range(n)]]
    return lax.all_to_all(msg, (axis, "gz"), 0, 0, tiled=True, axis_index_groups=groups)


def cost(us):
    return pl.CostEstimate(flops=0, bytes_accessed=int(us * 3.6e6), transcendentals=0)


def body(state, source, x_faces, y_faces, couple, omega):
    n_y = lax.axis_size("gy")
    pairs = [(i, i ^ 1) for i in range(n_y)]
    other_pairs = [(i, (i + 1) % n_y if i % 2 else (i - 1) % n_y) for i in range(n_y)]
    flip = [(0, 1), (1, 0)]
    field = sds(B, B, V, N, 128)
    mats = [scratch(25, 8, 128)] * 3 + [scratch(40, 8, 128)] + [scratch(25, 8, 128)] * 3

    couple = jnp.transpose(couple, (0, 2, 3, 1, 4))
    x_faces = jnp.transpose(x_faces, (0, 1, 3, 2, 4))
    y_faces = jnp.transpose(y_faces, (0, 1, 3, 2, 4))
    rows = jnp.transpose(state, (0, 2, 3, 1, 4)).reshape(LINE, 128)
    near, far = call(edge_kernel, [vmem], [sds(B, V, N, 128), sds(B, V, N, 128)])(rows)
    near = lax.ppermute(near, "gy", pairs)
    far = lax.ppermute(far, "gy", other_pairs)
    fac, xmat, ymat, tail, edge, table = call(
        matrix_kernel, [smem] + [vmem] * 4,
        [
            sds(225, 8, 128), sds(16 * MR, 128), sds(16 * YM, 128), sds(9, 8, 128), sds(N, 128),
            sds(N, N, 128),
        ],
        [scratch(2 * B * 25 * 8, 128)] + [scratch(2 * B * V * 8, 128)] * 2,
        cost_estimate=cost(1),
    )(omega, state, couple, x_faces, y_faces)
    halo = lax.ppermute(edge, "gz", flip)
    part = call(
        inner_kernel, [vmem] * 4, field, cost_estimate=cost(1)
    )(state, source, y_faces, table)
    r1, v, msg = call(
        first_kernel, [vmem] * 8,
        [field, sds(B - 1, B, V, N, 128), sds(16, XR, 128)],
    )(part, near, far, halo, x_faces, y_faces, fac, xmat)
    got = exchange(msg, "gx")
    mats += [scratch(25, 8, 128)] * 2
    ret = call(x_solver_kernel, [vmem], sds(16 * 40, 128), mats)(got.reshape(16 * XR, 128))
    back = exchange(ret.reshape(16, 40, 128), "gx")
    h, edge = call(middle_kernel, [vmem] * 3, [field, sds(N, 128)])(back, v, fac)
    halo = lax.ppermute(edge, "gz", flip)
    part = call(
        second_inner_kernel, [vmem] * 5, field, cost_estimate=cost(1)
    )(h, source, r1, couple, table)
    v, msg = call(
        second_kernel, [vmem] * 6, [sds(B, B - 1, V, N, 128), sds(8, YR, 128)]
    )(part, halo, y_faces, fac, ymat, tail)
    got = exchange(msg, "gy")
    ret = call(
        y_solver_kernel, [vmem], sds(8 * 80, 128), mats
    )(got.reshape(8 * YR, 128))
    back = exchange(ret.reshape(8, 80, 128), "gy")
    out = call(last_kernel, [vmem] * 3, sds(LINE, 128))(back, v, fac)
    return jnp.transpose(out.reshape(B, V, N, B, 128), (0, 3, 1, 2, 4))


def solution(mesh):
    return jax.shard_map(
        body,
        mesh=mesh,
        in_specs=(
            P("gx", "gy", None, None, "gz"),
            P("gx", "gy", None, None, "gz"),
            P(None, "gx", "gy", None, "gz"),
            P(None, "gx", "gy", None, "gz"),
            P("gx", "gy", None, None, "gz"),
            P(),
        ),
        out_specs=P("gx", "gy", None, None, "gz"),
        check_vma=False,
    )
```

```python
import functools
import math

import jax
import jax.numpy as jnp
from jax import lax
from jax.experimental import pallas as pl
from jax.experimental.pallas import tpu as pltpu
from jax.sharding import PartitionSpec as P


V = 5
N = 15
B = 4
H = 8
XR = 96
MR = 56
YR = 128
YM = 48
LINE = B * V * N * B
f32 = jnp.float32


def spectral_entry(gap):
    return 0.0 if gap == 0 else 0.5 * (-1) ** gap / math.sin(math.pi * gap / N)


def spectral_table(omega, table):
    subs = sub((N, 128))
    entries = {gap: omega * spectral_entry(gap) for gap in range(1 - N, N)}
    for k in range(N):
        column = jnp.zeros((N, 128), f32)
        for j in range(N):
            column = jnp.where(subs == j, entries[j - k], column)
        table[k] = column


def lane(shape=(8, 128)):
    return lax.broadcasted_iota(jnp.int32, shape, len(shape) - 1)


def sub(shape=(8, 128)):
    return lax.broadcasted_iota(jnp.int32, shape, len(shape) - 2)


def swap(v):
    return pltpu.roll(v, 64, 1)


def split(e0, e1):
    far, left = swap(e1), lane() < 64
    return jnp.where(left, e0, far), jnp.where(left, far, e0)


def join(z0, z1):
    left = lane() < 64
    return jnp.where(left, z0, z1), swap(jnp.where(left, z1, z0))


def choose(flag, p, q):
    return jnp.where(flag, q, p), jnp.where(flag, p, q)


def inverse(m):
    m = list(m)
    for p in range(V):
        piv = 1.0 / m[p * V + p]
        for j in range(V):
            if j != p:
                m[p * V + j] = m[p * V + j] * piv
        m[p * V + p] = piv
        for i in range(V):
            if i != p:
                f = m[i * V + p]
                for j in range(V):
                    if j != p:
                        m[i * V + j] = m[i * V + j] - f * m[p * V + j]
                m[i * V + p] = -f * piv
    return m


def dot(terms):
    total = None
    for a, b in terms:
        total = a * b if total is None else total + a * b
    return total


def matmul(a, b):
    return [
        dot([(a[i * V + k], b[k * V + j]) for k in range(V)]) for i in range(V) for j in range(V)
    ]


def edge_kernel(state_ref, near_ref, far_ref):
    even = lax.axis_index("gy") % 2 == 0

    def line(at):
        p = state_ref[pl.ds(at, H, stride=B), :]
        q = state_ref[pl.ds(at + (N - H) * B, H, stride=B), :]
        return jnp.concatenate([p, q[2 * H - N :]], axis=0)

    for x in range(B):
        for i in range(V):
            at = (x * V + i) * N * B
            first, last = line(at), line(at + B - 1)
            near_ref[x, i], far_ref[x, i] = choose(even, first, last)


def pack_edges(load, flag):
    shift = jnp.where(flag == 0, 1, 0)
    lanes = lane((N, 128))
    acc = jnp.zeros((N, 128), f32)
    for c in range(B * B * V):
        x, y, i = c // (B * V), (c // V) % B, c % V
        acc = jnp.where(lanes == c, pltpu.roll(load(x, y, i), shift + c, 1), acc)
    return acc


def z_inner(v, lanes):
    low = jnp.where(lanes == 0, 0.0, pltpu.roll(v, 1, 1))
    high = jnp.where(lanes == 127, 0.0, pltpu.roll(v, 127, 1))
    return low + high


def z_outer(halo, c, flag, lanes):
    edge = jnp.where(flag == 0, 127, 0)
    shift = jnp.where(flag == 0, 127 - c, 128 - c)
    return jnp.where(lanes == edge, pltpu.roll(halo, shift, 1), 0.0)


def matrix_kernel(
    omega_ref, state_ref, couple_ref, xf_ref, yf_ref, fac_ref, xmat_ref, ymat_ref, tail_ref,
    edge_ref, table_ref, mel, lo, hi,
):
    spectral_table(omega_ref[0], table_ref)
    edge_ref[...] = pack_edges(lambda x, y, i: state_ref[x, y, i], lax.axis_index("gz"))
    for a in range(B):
        for i in range(V):
            for j in range(V):
                c = couple_ref[a, i, j]
                e = i * V + j
                mel[(a * 25 + e) * 8 : (a * 25 + e) * 8 + 4, :] = c
                mel[pl.ds(e * 8 + 4 + a, B, stride=25 * 8), :] = c
            lo[(a * V + i) * 8 : (a * V + i) * 8 + 4, :] = xf_ref[0, a, i]
            hi[(a * V + i) * 8 : (a * V + i) * 8 + 4, :] = xf_ref[1, a, i]
            lo[pl.ds(i * 8 + 4 + a, B, stride=V * 8), :] = yf_ref[0, a, i]
            hi[pl.ds(i * 8 + 4 + a, B, stride=V * 8), :] = yf_ref[1, a, i]

    def row(ref, r):
        return ref[r * 8 : r * 8 + 8, :]

    low = [[row(lo, t * V + i) for i in range(V)] for t in range(B)]
    high = [[row(hi, t * V + i) for i in range(V)] for t in range(B)]

    def mid(t):
        m = [row(mel, t * 25 + e) for e in range(25)]
        for i in range(V):
            m[i * V + i] = m[i * V + i] + (low[t][i] + high[t][i])
        return m

    def put(block, m):
        for e in range(25):
            fac_ref[block * 25 + e] = m[e]

    def get(block):
        return [fac_ref[block * 25 + e] for e in range(25)]

    def rows_by(d, m):
        return [d[i] * m[i * V + j] for i in range(V) for j in range(V)]

    def cols_by(m, d):
        return [m[i * V + j] * d[j] for i in range(V) for j in range(V)]

    g0 = inverse(mid(0))
    put(0, g0)
    m1 = mid(1)
    s = rows_by(low[1], cols_by(g0, high[0]))
    g1 = inverse([p - q for p, q in zip(m1, s)])
    put(1, g1)
    m2 = mid(2)
    s = rows_by(low[2], cols_by(g1, high[1]))
    g2 = inverse([p - q for p, q in zip(m2, s)])
    put(2, g2)
    e2 = cols_by(g2, high[2])
    put(8, e2)
    e1 = matmul(get(1), rows_by(high[1], e2))
    put(7, e1)
    e0 = matmul(get(0), rows_by(high[0], e1))
    put(6, e0)
    l0 = cols_by(get(0), low[0])
    l1 = matmul(get(1), rows_by(low[1], l0))
    l2 = matmul(get(2), rows_by(low[2], l1))
    put(5, l2)
    b1 = matmul(get(1), rows_by(high[1], l2))
    l1 = [p + q for p, q in zip(l1, b1)]
    put(4, l1)
    b0 = matmul(get(0), rows_by(high[0], l1))
    l0 = [p + q for p, q in zip(cols_by(get(0), low[0]), b0)]
    put(3, l0)

    lanes = lane()
    m3 = mid(3)
    last_low, last_high = get(5), get(8)
    first_low, first_high = get(3), get(6)

    blocks = [[], [], [], []]
    for i in range(V):
        for j in range(V):
            e = i * V + j
            blocks[0].append(-(low[3][i] * last_low[e]))
            blocks[1].append(m3[e] - low[3][i] * last_high[e])
            blocks[2].append(first_low[e])
            blocks[3].append(first_high[e])
    zero = jnp.zeros((8, 128), f32)
    edge = [high[3][i] for i in range(V)]
    odd = lax.axis_index("gx") % 2 == 1
    for r in range(55):
        if r < 50:
            e0, e1 = blocks[0 if r < 25 else 1][r % 25], blocks[3 if r < 25 else 2][r % 25]
        else:
            e0, e1 = edge[r - 50], zero
        for zh, v in enumerate(split(*choose(odd, e0, e1))):
            xmat_ref[pl.ds(zh * MR + r, 4, stride=2 * MR), :] = v[0:4]
        if r % 25 < 24 and r < 50:
            for zh, v in enumerate(split(e0, e1)):
                at = zh * YM + r - r // 25
                ymat_ref[pl.ds(at, 4, stride=2 * YM), :] = v[4:8]
    for d in range(8):
        xmat_ref[d * MR + 55 : (d + 1) * MR, :] = jnp.zeros((1, 128), f32)
    for k, e in enumerate(edge + [blocks[0][24], blocks[3][24], blocks[1][24], blocks[2][24]]):
        tail_ref[k] = e


def halves(v, tail=None):
    tail = jnp.zeros((1, 128), f32) if tail is None else tail
    return v[0:H], jnp.concatenate([v[H:N], tail], axis=0)


def apply(fac_ref, block, line, vec):
    out = []
    for i in range(V):
        out.append(
            dot([(fac_ref[block * 25 + i * V + k, line : line + 1, :], vec[k]) for k in range(V)])
        )
    return out


def condense(fac_ref, line, right, low, high):
    y0 = apply(fac_ref, 0, line, right(0))
    y1 = apply(fac_ref, 1, line, [r + l * y for r, l, y in zip(right(1), low(1), y0)])
    v2 = apply(fac_ref, 2, line, [r + l * y for r, l, y in zip(right(2), low(2), y1)])
    c1 = apply(fac_ref, 1, line, [h * v for h, v in zip(high(1), v2)])
    v1 = [p + q for p, q in zip(y1, c1)]
    c0 = apply(fac_ref, 0, line, [h * v for h, v in zip(high(0), v1)])
    v0 = [p + q for p, q in zip(y0, c0)]
    last = [r + l * v for r, l, v in zip(right(3), low(3), v2)]
    return v0, v1, v2, last


def spectral_terms(load, table, lanes_shape=(N, 128)):
    acc = [None] * V
    for k in range(N):
        t = table[k]
        for i in range(V):
            p = t * load(i, k)
            acc[i] = p if acc[i] is None else acc[i] + p
    return acc


def inner_kernel(state_ref, source_ref, yf_ref, table, r_ref):
    lanes = lane((N, 128))
    for y in range(B):
        for x in range(B):
            spec = spectral_terms(lambda i, k: state_ref[x, y, i, k : k + 1, :], table)
            for i in range(V):
                s = state_ref[x, y, i]
                yl = yf_ref[0, x, i, y : y + 1, :]
                yh = yf_ref[1, x, i, y : y + 1, :]
                r = source_ref[x, y, i] - (yl + yh + 1.0) * s + 0.5 * z_inner(s, lanes)
                if y > 0:
                    r = r + yl * state_ref[x, y - 1, i]
                if y < B - 1:
                    r = r + yh * state_ref[x, y + 1, i]
                r_ref[x, y, i] = r - spec[i]


def first_kernel(
    part_ref, near_ref, far_ref, halo_ref, xf_ref, yf_ref, fac_ref, xmat_ref,
    r_ref, v_ref, msg_ref,
):
    flag = lax.axis_index("gz")
    lanes = lane((N, 128))
    halo = halo_ref[...]
    at = lax.axis_index("gy")
    even, begin, end = at % 2 == 0, at == 0, at == lax.axis_size("gy") - 1
    odd = lax.axis_index("gx") % 2 == 1
    for y in range(B):
        for x in range(B):
            for i in range(V):
                r = part_ref[x, y, i] + 0.5 * z_outer(halo, (x * B + y) * V + i, flag, lanes)
                if y == 0:
                    below = jnp.where(even, far_ref[x, i], near_ref[x, i])
                    r = r + yf_ref[0, x, i, y : y + 1, :] * jnp.where(begin, 0.0, below)
                if y == B - 1:
                    above = jnp.where(even, near_ref[x, i], far_ref[x, i])
                    r = r + yf_ref[1, x, i, y : y + 1, :] * jnp.where(end, 0.0, above)
                r_ref[x, y, i] = r
    for y in range(B):
        v0, v1, v2, last = condense(
            fac_ref, y,
            lambda t: [r_ref[t, y, i] for i in range(V)],
            lambda t: [xf_ref[0, t, i, y : y + 1, :] for i in range(V)],
            lambda t: [xf_ref[1, t, i, y : y + 1, :] for i in range(V)],
        )
        for i in range(V):
            v_ref[0, y, i] = v0[i]
            v_ref[1, y, i] = v1[i]
            v_ref[2, y, i] = v2[i]
            for ih, (e0, e1) in enumerate(zip(halves(last[i]), halves(v0[i]))):
                for zh, v in enumerate(split(*choose(odd, e0, e1))):
                    msg_ref[y * 4 + zh * 2 + ih, i * H : (i + 1) * H, :] = v
    for d in range(16):
        msg_ref[d, 40:XR, :] = xmat_ref[d // 2 * MR : (d // 2 + 1) * MR, :]


def product(a, m):
    out = []
    for i in range(V):
        row = [a[i * V + k] for k in range(V)]
        out += [dot([(row[k], m[k * V + j]) for k in range(V)]) for j in range(V)]
    return out


def reduce_lines(a, b, c, r, prepare, before, after, far, steps, kk, nn, bi, lower):
    def invert():
        inv = inverse([b[e] for e in range(25)])
        for e in range(25):
            bi[e] = inv[e]

    def put(dst, m, sign=1):
        for e in range(25):
            dst[e] = m[e] if sign > 0 else -m[e]

    def subtract(m):
        for e in range(25):
            b[e] = b[e] - m[e]

    for step in range(steps - 1):
        k = 2**step

        def low(m):
            return [before(v, k) for v in m]

        def high(m):
            return [after(v, k) for v in m]

        invert()
        m = [prepare(bi[e], k) for e in range(25)]
        put(kk, product(a, low(m)))
        put(nn, product(c, high(m)))
        for n in range(H):
            old = [r[i * H + n] for i in range(V)]
            m = [prepare(v, k) for v in old]
            m = low(m), high(m)
            for i in range(V):
                r[i * H + n] = (
                    old[i]
                    - dot([(kk[i * V + q], m[0][q]) for q in range(V)])
                    - dot([(nn[i * V + q], m[1][q]) for q in range(V)])
                )
        m = [prepare(c[e], k) for e in range(25)]
        subtract(product(kk, low(m)))
        put(c, product(nn, high(m)), -1)
        m = [prepare(a[e], k) for e in range(25)]
        subtract(product(nn, high(m)))
        put(a, product(kk, low(m)), -1)
    invert()
    for e in range(25):
        a[e] = jnp.where(lower, c[e], a[e])
    put(kk, product(a, [far(bi[e]) for e in range(25)]))
    for n in range(H):
        old = [r[i * H + n] for i in range(V)]
        other = [far(v) for v in old]
        for i in range(V):
            r[i * H + n] = old[i] - dot([(kk[i * V + q], other[q]) for q in range(V)])
    subtract(product(kk, [far(a[e]) for e in range(25)]))
    invert()
    for n in range(H):
        old = [r[i * H + n] for i in range(V)]
        for i in range(V):
            r[i * H + n] = dot([(bi[i * V + q], old[q]) for q in range(V)])


def places():
    return (sub() + 4 * lax.axis_index("gz")) % 8


def close(b, c, fl, fh, edge):
    for i in range(V):
        for j in range(V):
            e = i * V + j
            c[e] = -(edge[i] * fh[e])
            b[e] = b[e] - edge[i] * fl[e]


def x_solver_kernel(msg_ref, out_ref, a, b, c, r, kk, nn, bi, fh, fl):
    lanes, subs = lane(), places()
    even = lanes < 64
    even = jnp.logical_xor(even, lax.axis_index("gx") // 2 % 2 == 1)

    def pair(row):
        return [msg_ref[pl.ds(row + p * XR, 8, stride=2 * XR), :] for p in range(2)]

    def own(p, q):
        return jnp.where(even, p, q)

    def following(p, q):
        v = jnp.where(even, q, p)
        return jnp.where(even, v, pltpu.roll(v, 7, 0))

    def prepare(v, k):
        return swap(v) if k == 1 else v

    def before(v, k):
        if k > 1:
            return pltpu.roll(v, k // 2, 0)
        return jnp.where(even, pltpu.roll(v, 1, 0), v)

    def after(v, k):
        if k > 1:
            return pltpu.roll(v, 8 - k // 2, 0)
        return jnp.where(even, v, pltpu.roll(v, 7, 0))

    def far(v):
        return pltpu.roll(v, 4, 0)

    begin = (subs == 0) & even
    end = (subs == 7) & jnp.logical_not(even)
    for e in range(25):
        p, q = pair(40 + e)
        a[e], fh[e] = jnp.where(begin, 0.0, own(p, q)), following(p, q)
        p, q = pair(65 + e)
        b[e], fl[e] = own(p, q), following(p, q)
    edge = [jnp.where(end, 0.0, own(*pair(90 + i))) for i in range(V)]
    close(b, c, fl, fh, edge)
    for e in range(40):
        p, q = pair(e)
        r[e] = own(p, q) + edge[e // H] * following(p, q)
    reduce_lines(a, b, c, r, prepare, before, after, far, 4, kk, nn, bi, subs < 4)
    for e in range(40):
        u = r[e]
        v = swap(u)
        before = jnp.where(subs == 0, 0.0, pltpu.roll(v, 1, 0))
        out_ref[pl.ds(e, 8, stride=80), :] = jnp.where(even, before, v)
        out_ref[pl.ds(40 + e, 8, stride=80), :] = u


def y_solver_kernel(msg_ref, out_ref, a, b, c, r, kk, nn, bi, fh, fl):
    lanes, subs = lane(), places()
    left = jnp.logical_xor(lanes < 64, lax.axis_index("gy") % 2 == 1)

    def rhs(row):
        return msg_ref[pl.ds(row, 8, stride=YR), :]

    def following(v):
        return pltpu.roll(v, 7, 0)

    def pair(row):
        p = rhs(row)
        q = swap(p)
        return jnp.where(left, p, q), jnp.where(left, q, p)

    begin = subs == 0
    for e in range(24):
        low, high = pair(80 + e)
        a[e], fh[e] = jnp.where(begin, 0.0, low), following(high)
        b[e], high = pair(104 + e)
        fl[e] = following(high)

    def tail(row):
        return pair(row * H + H - 1)[1]

    a[24], fh[24] = jnp.where(begin, 0.0, tail(5)), following(tail(6))
    b[24], fl[24] = tail(7), following(tail(8))
    edge = [jnp.where(subs == 7, 0.0, tail(i)) for i in range(V)]
    close(b, c, fl, fh, edge)
    for e in range(40):
        r[e] = rhs(e) + edge[e // H] * following(rhs(40 + e))
    reduce_lines(
        a, b, c, r, lambda v, k: v, lambda v, k: pltpu.roll(v, k, 0),
        lambda v, k: pltpu.roll(v, 8 - k, 0), lambda v: pltpu.roll(v, 4, 0),
        3, kk, nn, bi, subs < 4,
    )
    for e in range(40):
        u = r[e]
        out_ref[pl.ds(e, 8, stride=80), :] = jnp.where(begin, 0.0, pltpu.roll(u, 1, 0))
        out_ref[pl.ds(40 + e, 8, stride=80), :] = u


def middle_kernel(ret_ref, v_ref, fac_ref, h_ref, edge_ref):
    for y in range(B):
        prev, cur = [], []
        for i in range(V):
            um, u = [], []
            for ih in range(2):
                z = [ret_ref[y * 4 + 2 * zh + ih, i * H : (i + 1) * H, :] for zh in range(2)]
                p, q = join(*z)
                um.append(p)
                u.append(q)
            prev.append(jnp.concatenate(um, axis=0)[:N])
            cur.append(jnp.concatenate(u, axis=0)[:N])
        for t in range(B - 1):
            lo = apply(fac_ref, 3 + t, y, prev)
            hi = apply(fac_ref, 6 + t, y, cur)
            for i in range(V):
                h_ref[t, y, i] = v_ref[t, y, i] + lo[i] + hi[i]
        for i in range(V):
            h_ref[B - 1, y, i] = cur[i]
    edge_ref[...] = pack_edges(lambda x, y, i: h_ref[x, y, i], lax.axis_index("gz"))


def second_inner_kernel(h_ref, source_ref, r_ref, couple_ref, table, part_ref):
    lanes = lane((N, 128))
    for x in range(B):
        for y in range(B):
            spec = spectral_terms(lambda i, k: h_ref[x, y, i, k : k + 1, :], table)
            h = [h_ref[x, y, i] for i in range(V)]
            for i in range(V):
                c = dot([(couple_ref[x, i, k, y : y + 1, :], h[k]) for k in range(V)])
                r = source_ref[x, y, i] - r_ref[x, y, i] + c
                part_ref[x, y, i] = r - h[i] + 0.5 * z_inner(h[i], lanes) - spec[i]


def second_kernel(part_ref, halo_ref, yf_ref, fac_ref, ymat_ref, tail_ref, v_ref, msg_ref):
    flag = lax.axis_index("gz")
    lanes = lane((N, 128))
    halo = halo_ref[...]

    def right(x, t, i):
        return part_ref[x, t, i] + 0.5 * z_outer(halo, (x * B + t) * V + i, flag, lanes)

    for x in range(B):
        v0, v1, v2, last = condense(
            fac_ref, 4 + x,
            lambda t: [right(x, t, i) for i in range(V)],
            lambda t: [yf_ref[0, x, i, t : t + 1, :] for i in range(V)],
            lambda t: [yf_ref[1, x, i, t : t + 1, :] for i in range(V)],
        )
        for i in range(V):
            v_ref[x, 0, i] = v0[i]
            v_ref[x, 1, i] = v1[i]
            v_ref[x, 2, i] = v2[i]
            for at, v, k in ((0, last[i], i), (40, v0[i], 5 + i)):
                tail = tail_ref[k, 4 + x : 5 + x, :] if k < 9 else None
                for zh, m in enumerate(split(*halves(v, tail))):
                    msg_ref[x * 2 + zh, at + i * H : at + (i + 1) * H, :] = m
    for d in range(8):
        msg_ref[d, 80:YR, :] = ymat_ref[d * YM : (d + 1) * YM, :]


def last_kernel(ret_ref, v_ref, fac_ref, w_ref):
    def put(x, y, i, v):
        at = (x * V + i) * N * B + y
        w_ref[pl.ds(at, H, stride=B), :] = v[:H]
        w_ref[pl.ds(at + (N - H) * B, H, stride=B), :] = v[N - H :]

    for x in range(B):
        prev, cur = [], []
        for i in range(V):
            for out, at in ((prev, 0), (cur, 40)):
                z = [ret_ref[x * 2 + zh, at + i * H : at + (i + 1) * H, :] for zh in range(2)]
                rows = join(*z)
                out.append(jnp.concatenate(rows, axis=0)[:N])
        for t in range(B - 1):
            lo = apply(fac_ref, 3 + t, 4 + x, prev)
            hi = apply(fac_ref, 6 + t, 4 + x, cur)
            for i in range(V):
                put(x, t, i, v_ref[x, t, i] + lo[i] + hi[i])
        for i in range(V):
            put(x, B - 1, i, cur[i])


smem = pl.BlockSpec(memory_space=pltpu.SMEM)
vmem = pl.BlockSpec(memory_space=pltpu.VMEM)


def sds(*shape):
    return jax.ShapeDtypeStruct(shape, f32)


def scratch(*shape):
    return pltpu.VMEM(shape, f32)


def call(kernel, ins, outs, scratches=(), **more):
    single = not isinstance(outs, (list, tuple))
    return pl.pallas_call(
        kernel,
        in_specs=list(ins),
        out_specs=vmem if single else [vmem] * len(outs),
        out_shape=outs,
        scratch_shapes=list(scratches),
        compiler_params=pltpu.CompilerParams(vmem_limit_bytes=40 * 2**20),
        **more,
    )


def exchange(msg, axis):
    n = lax.axis_size(axis)
    groups = [[2 * i for i in range(n)], [2 * ((i + n // 2) % n) + 1 for i in range(n)]]
    return lax.all_to_all(msg, (axis, "gz"), 0, 0, tiled=True, axis_index_groups=groups)


def cost(us):
    return pl.CostEstimate(flops=0, bytes_accessed=int(us * 3.6e6), transcendentals=0)


def body(state, source, x_faces, y_faces, couple, omega):
    n_y = lax.axis_size("gy")
    pairs = [(i, i ^ 1) for i in range(n_y)]
    other_pairs = [(i, (i + 1) % n_y if i % 2 else (i - 1) % n_y) for i in range(n_y)]
    flip = [(0, 1), (1, 0)]
    field = sds(B, B, V, N, 128)
    mats = [scratch(25, 8, 128)] * 3 + [scratch(40, 8, 128)] + [scratch(25, 8, 128)] * 3

    couple = jnp.transpose(couple, (0, 2, 3, 1, 4))
    x_faces = jnp.transpose(x_faces, (0, 1, 3, 2, 4))
    y_faces = jnp.transpose(y_faces, (0, 1, 3, 2, 4))
    rows = jnp.transpose(state, (0, 2, 3, 1, 4)).reshape(LINE, 128)
    near, far = call(edge_kernel, [vmem], [sds(B, V, N, 128), sds(B, V, N, 128)])(rows)
    near = lax.ppermute(near, "gy", pairs)
    far = lax.ppermute(far, "gy", other_pairs)
    fac, xmat, ymat, tail, edge, table = call(
        matrix_kernel, [smem] + [vmem] * 4,
        [
            sds(225, 8, 128), sds(16 * MR, 128), sds(16 * YM, 128), sds(9, 8, 128), sds(N, 128),
            sds(N, N, 128),
        ],
        [scratch(2 * B * 25 * 8, 128)] + [scratch(2 * B * V * 8, 128)] * 2,
        cost_estimate=cost(1),
    )(omega, state, couple, x_faces, y_faces)
    halo = lax.ppermute(edge, "gz", flip)
    part = call(
        inner_kernel, [vmem] * 4, field, cost_estimate=cost(1)
    )(state, source, y_faces, table)
    r1, v, msg = call(
        first_kernel, [vmem] * 8,
        [field, sds(B - 1, B, V, N, 128), sds(16, XR, 128)],
    )(part, near, far, halo, x_faces, y_faces, fac, xmat)
    got = exchange(msg, "gx")
    mats += [scratch(25, 8, 128)] * 2
    ret = call(x_solver_kernel, [vmem], sds(16 * 40, 128), mats)(got.reshape(16 * XR, 128))
    back = exchange(ret.reshape(16, 40, 128), "gx")
    h, edge = call(middle_kernel, [vmem] * 3, [field, sds(N, 128)])(back, v, fac)
    halo = lax.ppermute(edge, "gz", flip)
    part = call(
        second_inner_kernel, [vmem] * 5, field, cost_estimate=cost(1)
    )(h, source, r1, couple, table)
    v, msg = call(
        second_kernel, [vmem] * 6, [sds(B, B - 1, V, N, 128), sds(8, YR, 128)]
    )(part, halo, y_faces, fac, ymat, tail)
    got = exchange(msg, "gy")
    ret = call(
        y_solver_kernel, [vmem], sds(8 * 80, 128), mats
    )(got.reshape(8 * YR, 128))
    back = exchange(ret.reshape(8, 80, 128), "gy")
    out = call(last_kernel, [vmem] * 3, sds(LINE, 128))(back, v, fac)
    return jnp.transpose(out.reshape(B, V, N, B, 128), (0, 3, 1, 2, 4))


def solution(mesh):
    return jax.shard_map(
        body,
        mesh=mesh,
        in_specs=(
            P("gx", "gy", None, None, "gz"),
            P("gx", "gy", None, None, "gz"),
            P(None, "gx", "gy", None, "gz"),
            P(None, "gx", "gy", None, "gz"),
            P("gx", "gy", None, None, "gz"),
            P(),
        ),
        out_specs=P("gx", "gy", None, None, "gz"),
        check_vma=False,
    )
```
